32 devices in a mesh: enc: 4 (over z), mb: 2 (over core), tp: 4 (over y, x).
Axes of the slice: x: 2, y: 2, z: 4, core: 2. Of those that a mesh axis runs over, the one named last changes fastest.
Arguments:
- patches: bfloat16 [4, 2, 256, 1280], P('enc', 'mb', 'tp'), may hold values from -6 to 6
- patch_counts: int32 [4, 2, 8], P('enc', 'mb'), may hold values from 4 to 32, as said below
- dest_pos: int32 [4, 2, 64], P('enc', 'mb'), may hold values from 0 to 511, as said below
- merge_gain: float32 [1280], replicated, may hold values from 0.25 to 1.75
- merge_bias: float32 [1280], replicated, may hold values from -3 to 3
- up_weight: bfloat16 [5120, 5120], P(('enc', 'mb'), 'tp'), may hold values from -0.078125 to 0.078125
- up_bias: float32 [5120], replicated, may hold values from -3 to 3
- down_weight: bfloat16 [5120, 8192], P('tp', ('enc', 'mb')), may hold values from -0.078125 to 0.078125
- down_bias: float32 [8192], replicated, may hold values from -3 to 3
- text_embed: bfloat16 [4, 2, 512, 8192], P('enc', 'mb', 'tp'), may hold values from -6 to 6
- norm_gain: float32 [8192], replicated, may hold values from 0.25 to 1.75
- kv_weight: bfloat16 [8192, 2048], P('tp'), may hold values from -0.0625 to 0.0625
- kv_bias: float32 [2048], replicated, may hold values from -3 to 3
Outputs:
- embedded: bfloat16 [4, 2, 512, 8192], P('enc', 'mb', 'tp')
- keys_values: bfloat16 [4, 2, 512, 2048], P('enc', 'mb', 'tp')
The draws below stay inside these ranges and needn't reach their ends.
Inputs may be any that keep to these rules, and one draw needn't show every extreme that they name: `patch_counts`: each image's patch count is four times its merged rows; in every sequence some image has 32 patches. The image slots of enc index e and mb index m feed sequence (e, m); slot j of device t of tp is image t * 2 + j. `dest_pos`: the 8 slots of an image hold consecutive positions; slots past the image's merged rows are not live and their positions are used by no live slot; no two live slots of a sequence share a position.
All inputs are finite; a program needn't handle non-finite values.
Results may differ from the reference program's by a relative error of at most 0.02.
Values may be sent and summed in bfloat16 or wider, within the bound.
A program may use at most 128 MiB of HBM per device.

```python
import jax
import jax.numpy as jnp
from jax import lax

DV = 1280
MERGED = 5120
HID = 5120
D = 8192
KV_COLS = 2048
TOK_DEV = 128
IMG_DEV = 2
SLOT = 8
SLOTS_DEV = 16
GS = 64
SEQ = 512
N_ENC = 4
N_MB = 2
N_TP = 4


def image_layout(key):
    groups = N_ENC * N_MB
    images = N_TP * IMG_DEV
    segment = TOK_DEV // IMG_DEV
    keys = jax.random.split(key, 6)
    heavy = jax.random.randint(keys[0], (groups, N_TP, 1), 0, 2)
    broad = jax.random.randint(keys[1], (groups, N_TP, IMG_DEV), 1, SLOT + 1)
    slim = jax.random.randint(keys[2], (groups, N_TP, IMG_DEV), 1, max(SLOT // 4, 1) + 1)
    rows = jnp.where(heavy == 1, broad, slim).reshape(groups, images)
    filled = jax.random.randint(keys[3], (groups, 1), 0, images)
    rows = jnp.where(jnp.arange(images)[None, :] == filled, SLOT, rows)
    order = jax.vmap(lambda sub: jax.random.permutation(sub, images))(jax.random.split(keys[4], groups))
    offset = jax.random.randint(keys[5], (groups, images), 0, segment - SLOT + 1)
    first = order * segment + offset
    places = first[:, :, None] + jnp.arange(SLOT)[None, None, :]
    return (rows.astype(jnp.int32), places.reshape(groups, GS).astype(jnp.int32))


def draw_patch_counts(key, part):
    rows, places = image_layout(key)
    return (4 * rows).reshape(N_ENC, N_MB, N_TP * IMG_DEV)


def draw_dest_pos(key, part):
    rows, places = image_layout(key)
    return places.reshape(N_ENC, N_MB, GS)


def steps_of(rng, dims, cuts, least, top_value):
    loudness, own = 1.0, jax.random.fold_in(rng, 6)
    for position, blocks in cuts:
        heights = jnp.exp(jax.random.uniform(jax.random.fold_in(own, position), (blocks,), jnp.float32, least / len(cuts), top_value / len(cuts)))
        loudness = loudness * jnp.repeat(heights, dims[position] // blocks).reshape([-1 if axis == position else 1 for axis in range(len(dims))])
    return loudness


def gaussian(rng, extent, scale, reach, pieces=(), kind=jnp.bfloat16):
    drawn = scale * jax.random.normal(rng, extent, jnp.float32)
    if pieces:
        drawn = drawn * steps_of(rng, extent, pieces, -0.22, 0.18)
    return jnp.clip(drawn, -reach, reach).astype(kind)


def setup_inputs(seed: int = 0) -> dict:
    arg_keys = jax.random.split(jax.random.key(seed), 14)
    return {
        "patches": gaussian(arg_keys[0], (N_ENC, N_MB, N_TP * 4 * SLOTS_DEV, DV), 1.0, 6.0, ((0, 4), (1, 2), (2, 4))),
        "patch_counts": draw_patch_counts(jax.random.fold_in(arg_keys[13], 71), 0),
        "dest_pos": draw_dest_pos(jax.random.fold_in(arg_keys[13], 71), 0),
        "merge_gain": jnp.clip(1.0 + 0.15 * jax.random.normal(arg_keys[3], (DV,), jnp.float32), 0.25, 1.75),
        "merge_bias": gaussian(arg_keys[4], (DV,), 0.5, 3.0, (), jnp.float32),
        "up_weight": gaussian(arg_keys[5], (MERGED, HID), MERGED ** -0.5, 0.078125, ((0, 8), (1, 4))),
        "up_bias": gaussian(arg_keys[6], (HID,), 0.5, 3.0, (), jnp.float32),
        "down_weight": gaussian(arg_keys[7], (HID, D), HID ** -0.5, 0.078125, ((0, 4), (1, 8))),
        "down_bias": gaussian(arg_keys[8], (D,), 0.5, 3.0, (), jnp.float32),
        "text_embed": gaussian(arg_keys[9], (N_ENC, N_MB, SEQ, D), 1.0, 6.0, ((0, 4), (1, 2), (2, 4))),
        "norm_gain": jnp.clip(1.0 + 0.15 * jax.random.normal(arg_keys[10], (D,), jnp.float32), 0.25, 1.75),
        "kv_weight": gaussian(arg_keys[11], (D, KV_COLS), D ** -0.5, 0.0625, ((0, 4),)),
        "kv_bias": gaussian(arg_keys[12], (KV_COLS,), 0.5, 3.0, (), jnp.float32),
    }


def layer_norm(rows, gain, bias):
    values = rows.astype(jnp.float32)
    center = values - lax.optimization_barrier(jnp.mean(values, axis=-1, keepdims=True))
    spread = lax.optimization_barrier(jnp.mean(center * center, axis=-1, keepdims=True))
    return center * lax.rsqrt(spread + 1e-06) * gain + bias

def root_scale(values, gain):
    return (values * lax.rsqrt(lax.optimization_barrier(jnp.mean(values * values, axis=-1, keepdims=True)) + 1e-06) * gain).astype(jnp.bfloat16)

def block_sum(left, right, blocks):
    width = left.shape[1] // blocks

    def step(total, block):
        start = (block * width).astype(jnp.int32)
        piece = lax.dynamic_slice_in_dim(left, start, width, 1)
        rows = lax.dynamic_slice_in_dim(right, start, width, 0)
        term = jnp.dot(piece, rows, preferred_element_type=jnp.float32)
        term = lax.optimization_barrier(term.astype(jnp.bfloat16)).astype(jnp.float32)
        return (total + term, 0)
    empty = jnp.zeros((left.shape[0], right.shape[1]), jnp.float32)
    total, unused = lax.scan(step, empty, jnp.arange(blocks, dtype=jnp.int32))
    return total

def reference(patches, patch_counts, dest_pos, merge_gain, merge_bias, up_weight, up_bias, down_weight, down_bias, text_embed, norm_gain, kv_weight, kv_bias):
    groups = N_ENC * N_MB
    patch_all = patches.reshape(groups, 4 * GS, DV)
    count_all = patch_counts.reshape(groups, N_TP * IMG_DEV)
    place_all = dest_pos.reshape(groups, GS)
    text_all = text_embed.reshape(groups, SEQ, D)

    def one_group(inputs):
        patch, counts, places, text = inputs
        normal = layer_norm(patch, merge_gain, merge_bias).astype(jnp.bfloat16)
        merged = normal.reshape(GS, MERGED)
        raised = jnp.dot(merged, up_weight, preferred_element_type=jnp.float32) + up_bias
        hidden = jax.nn.gelu(raised, approximate=False).astype(jnp.bfloat16)
        total = block_sum(hidden, down_weight, N_TP) + down_bias
        visual = total.astype(jnp.bfloat16)
        live_rows = counts // 4
        live = (jnp.arange(SLOT, dtype=jnp.int32)[None, :] < live_rows[:, None]).reshape(GS)
        target = jnp.where(live, places, SEQ).astype(jnp.int32)
        embedded = text.at[target].set(visual, mode='drop')
        normed = root_scale(embedded.astype(jnp.float32), norm_gain)
        kv_total = block_sum(normed, kv_weight, N_TP) + kv_bias
        return (embedded, kv_total.astype(jnp.bfloat16))
    embedded, keys_values = lax.map(one_group, (patch_all, count_all, place_all, text_all))
    return (embedded.reshape(N_ENC, N_MB, SEQ, D), keys_values.reshape(N_ENC, N_MB, SEQ, KV_COLS))
```

```python
import jax
import jax.numpy as jnp
from jax import lax
from jax.sharding import PartitionSpec as P

SLOT = 8
GROUP = ("enc", "mb")


def layer_norm(rows, gain, bias):
    values = rows.astype(jnp.float32)
    center = values - jnp.mean(values, axis=-1, keepdims=True)
    spread = jnp.mean(center * center, axis=-1, keepdims=True)
    return center * lax.rsqrt(spread + 1e-06) * gain + bias


def per_device(
    patches,
    patch_counts,
    dest_pos,
    merge_gain,
    merge_bias,
    up_weight,
    up_bias,
    down_weight,
    down_bias,
    text_embed,
    norm_gain,
    kv_weight,
    kv_bias,
):
    groups = lax.axis_size("enc") * lax.axis_size("mb")
    parts = lax.axis_size("tp")
    tp = lax.axis_index("tp")
    group = lax.axis_index("enc") * lax.axis_size("mb") + lax.axis_index("mb")
    text = text_embed[0, 0]
    tokens, width = text.shape
    feats = kv_weight.shape[0]
    units = up_weight.shape[1]
    cols = down_weight.shape[1]
    own_gain = lax.dynamic_slice_in_dim(norm_gain, tp * feats, feats, 0)

    text_cols = lax.all_to_all(text, "tp", split_axis=1, concat_axis=0, tiled=True)
    scaled = (text_cols.astype(jnp.float32) * own_gain).astype(jnp.bfloat16)
    text_part = jnp.dot(scaled, kv_weight, preferred_element_type=jnp.float32).astype(jnp.bfloat16)
    text_kv = lax.psum_scatter(text_part, "tp", scatter_dimension=0, tiled=True)

    normal = layer_norm(patches[0, 0], merge_gain, merge_bias).astype(jnp.bfloat16)
    own = normal.shape[0] // 4
    merged = normal.reshape(own, normal.shape[1] * 4)
    slices = lax.all_to_all(merged, GROUP, split_axis=1, concat_axis=0, tiled=True)
    rows = lax.all_gather(slices, "tp", axis=0, tiled=True)
    raised = jnp.dot(rows, up_weight, preferred_element_type=jnp.float32).astype(jnp.bfloat16)
    raised = raised.reshape(parts, groups, own, units).transpose(1, 0, 2, 3).reshape(-1, units)
    raised = lax.psum_scatter(raised, GROUP, scatter_dimension=0, tiled=True).astype(jnp.float32)
    own_bias = lax.dynamic_slice_in_dim(up_bias, tp * units, units, 0)
    hidden = jax.nn.gelu(raised + own_bias, approximate=False).astype(jnp.bfloat16)
    all_hidden = lax.all_gather(hidden, GROUP, axis=0, tiled=True)
    lowered = jnp.dot(all_hidden, down_weight, preferred_element_type=jnp.float32).astype(jnp.bfloat16)
    lowered = lowered.reshape(groups, parts, own, cols).transpose(1, 0, 2, 3).reshape(-1, cols)
    lowered = lax.psum_scatter(lowered, "tp", scatter_dimension=0, tiled=True).astype(jnp.float32)
    down_own = lax.dynamic_slice_in_dim(down_bias, group * cols, cols, 0)
    visual = (lowered + down_own).astype(jnp.bfloat16)
    visual = lax.all_to_all(visual, GROUP, split_axis=0, concat_axis=1, tiled=True)
    visual_all = lax.all_gather(visual, "tp", axis=0, tiled=True)

    visual_cols = lax.dynamic_slice_in_dim(visual_all, tp * feats, feats, 1)
    visual_scaled = (visual_cols.astype(jnp.float32) * own_gain).astype(jnp.bfloat16)
    visual_part = jnp.dot(visual_scaled, kv_weight, preferred_element_type=jnp.float32).astype(jnp.bfloat16)
    visual_kv = lax.psum(visual_part, "tp")

    live_rows = patch_counts[0, 0] // 4
    live = (jnp.arange(SLOT, dtype=jnp.int32)[None, :] < live_rows[:, None]).reshape(-1)
    places = tp * tokens + jnp.arange(tokens, dtype=jnp.int32)
    select = (dest_pos[0, 0][None, :] == places[:, None]) & live[None, :]
    picks = select.astype(jnp.bfloat16)
    present = jnp.any(select, axis=1)[:, None]
    picked = jnp.dot(picks, visual_all, preferred_element_type=jnp.float32).astype(jnp.bfloat16)
    embedded = jnp.where(present, picked, text)
    values = embedded.astype(jnp.float32)
    scale = lax.rsqrt(jnp.mean(values * values, axis=-1, keepdims=True) + 1e-06)
    picked_kv = jnp.dot(picks, visual_kv, preferred_element_type=jnp.float32)
    kv_total = jnp.where(present, picked_kv, text_kv.astype(jnp.float32)) * scale
    keys_values = (kv_total + kv_bias).astype(jnp.bfloat16)
    return (embedded[None, None], keys_values[None, None])


def solution(mesh):
    return jax.shard_map(
        per_device,
        mesh=mesh,
        in_specs=(
            P("enc", "mb", "tp", None),
            P("enc", "mb", None),
            P("enc", "mb", None),
            P(),
            P(),
            P(("enc", "mb"), "tp"),
            P(),
            P("tp", ("enc", "mb")),
            P(),
            P("enc", "mb", "tp", None),
            P(),
            P("tp", None),
            P(),
        ),
        out_specs=(P("enc", "mb", "tp", None), P("enc", "mb", "tp", None)),
        check_vma=False,
    )
```

```python
import functools

import jax
import jax.numpy as jnp
from jax import lax
from jax.experimental import pallas as pl
from jax.experimental.pallas import tpu as pltpu
from jax.sharding import PartitionSpec as P

SLOT = 8
F32 = jnp.float32
BF16 = jnp.bfloat16
MESH = pl.DeviceIdType.MESH


def tiles(width, tile):
    return tile if width % tile == 0 else width


def kernel(
    dims,
    patches,
    merge_gain,
    merge_bias,
    up_bias,
    down_bias,
    gain_col,
    kv_bias,
    picks,
    present,
    up_hbm,
    down_hbm,
    kv_hbm,
    text_hbm,
    embedded,
    keys_values,
    up_w,
    down_w,
    kv_w,
    text,
    split,
    rows,
    part,
    pair,
    chip_sum,
    summed,
    hidden,
    lowered,
    low_in,
    vis_part,
    visual,
    vkv,
    vkv_in,
    vkv_all,
    text_cols,
    text_part,
    text_in,
    local_sem,
    send_a,
    recv_a,
    send_b,
    recv_b,
    send_pair,
    recv_pair,
    send_c,
    recv_c,
    send_d,
    recv_d,
    send_fw,
    recv_fw,
    send_e,
    recv_e,
    send_f,
    recv_f,
    send_g,
    recv_g,
    send_h,
    recv_h,
    send_i,
    recv_i,
    send_t,
    recv_t,
    send_u,
    recv_u,
):
    n_enc, n_tp = dims
    groups = 2 * n_enc
    enc, mb, tp = lax.axis_index("enc"), lax.axis_index("mb"), lax.axis_index("tp")
    me = enc * 2 + mb
    own, kw = split.shape[1], split.shape[2]
    units = up_w.shape[1]
    cols = down_w.shape[1]
    feats, kv_cols = kv_w.shape
    tokens = text.shape[0]
    seq_rows = n_tp * own
    per_feat = feats // cols

    def other_groups():
        for step in range(1, groups):
            to = lax.rem(me + step, groups)
            yield to, {"enc": lax.div(to, 2), "mb": lax.rem(to, 2)}

    def other_encs():
        for step in range(1, n_enc):
            to = lax.rem(enc + step, n_enc)
            yield to, {"enc": to}

    def other_tps():
        for step in range(1, n_tp):
            to = lax.rem(tp + step, n_tp)
            yield to, {"tp": to}

    mate = {"mb": 1 - mb}

    def remote(src, dst, send, recv, to):
        return pltpu.make_async_remote_copy(
            src_ref=src, dst_ref=dst, send_sem=send, recv_sem=recv, device_id=to, device_id_type=MESH
        )

    local = [
        pltpu.make_async_copy(src, dst, local_sem.at[i])
        for i, (src, dst) in enumerate(
            ((up_hbm, up_w), (down_hbm, down_w), (kv_hbm, kv_w), (text_hbm, text))
        )
    ]
    for copy in local:
        copy.start()

    barrier = pltpu.get_barrier_semaphore()
    for _, to in other_groups():
        pl.semaphore_signal(barrier, inc=1, device_id=to, device_id_type=MESH)
    for _, to in other_tps():
        pl.semaphore_signal(barrier, inc=1, device_id=to, device_id_type=MESH)

    gain, bias = merge_gain[...], merge_bias[...]
    width = patches.shape[2]
    for j in range(4):
        values = patches[j].astype(F32)
        center = values - jnp.mean(values, axis=-1, keepdims=True)
        spread = jnp.mean(center * center, axis=-1, keepdims=True)
        normal = (center * lax.rsqrt(spread + 1e-06) * gain + bias).astype(BF16)
        for piece in range(width // kw):
            split[j * (width // kw) + piece] = normal[:, piece * kw : (piece + 1) * kw]
    pl.semaphore_wait(barrier, groups - 1 + n_tp - 1)

    copies_a = []
    for to, where in other_groups():
        copy = remote(split.at[to], rows.at[me, tp], send_a.at[to], recv_a.at[me], where)
        copy.start()
        copies_a.append(copy)
    rows[me, tp] = split[me]
    for at, where in other_groups():
        remote(split.at[at], rows.at[at, tp], send_a.at[at], recv_a.at[at], where).wait_recv()
    copies_b = []
    for to, where in other_tps():
        copy = remote(rows.at[:, tp], rows.at[:, tp], send_b.at[to], recv_b.at[tp], where)
        copy.start()
        copies_b.append(copy)

    copies_t = []
    for to, where in other_tps():
        copy = remote(
            text_hbm.at[:, pl.ds(pl.multiple_of(to * feats, feats), feats)],
            text_cols.at[tp],
            send_t.at[to],
            recv_t.at[tp],
            where,
        )
        copy.start()
        copies_t.append(copy)

    local[0].wait()
    for at, where in other_tps():
        remote(rows.at[:, at], rows.at[:, at], send_b.at[at], recv_b.at[at], where).wait_recv()

    tile = tiles(units, 256)

    @pl.loop(0, units // tile)
    def _(i):
        at = pl.ds(pl.multiple_of(i * tile, tile), tile)
        lhs = rows[...].reshape(groups * seq_rows, kw)
        out = jnp.dot(lhs, up_w[:, at], preferred_element_type=F32)
        part[:, :, :, at] = out.astype(BF16).reshape(n_enc, 2, seq_rows, tile)

    to_pair = remote(part.at[:, 1 - mb], pair, send_pair, recv_pair, mate)
    to_pair.start()
    to_pair.wait_recv()
    copies_c = []
    for to, where in other_encs():
        chip_sum[to] = (part[to, mb].astype(F32) + pair[to].astype(F32)).astype(BF16)
        copy = remote(chip_sum.at[to], summed.at[enc], send_c.at[to], recv_c.at[enc], where)
        copy.start()
        copies_c.append(copy)

    local[2].wait()

    @pl.loop(0, feats // 128)
    def _(i):
        at = pl.ds(pl.multiple_of(i * 128, 128), 128)
        kv_w[at, :] = (kv_w[at, :].astype(F32) * gain_col[at, :]).astype(BF16)

    local[3].wait()
    text_cols[tp] = text[:, pl.ds(pl.multiple_of(tp * feats, feats), feats)]

    total = part[enc, mb].astype(F32) + pair[enc].astype(F32) + up_bias[...]
    for at, where in other_encs():
        remote(chip_sum.at[at], summed.at[at], send_c.at[at], recv_c.at[at], where).wait_recv()
        total = total + summed[at].astype(F32)
    hidden[enc, mb] = (0.5 * total * (1.0 + lax.erf(total * 0.7071067811865476))).astype(BF16)

    copies_d = []
    copy = remote(hidden.at[enc, mb], hidden.at[enc, mb], send_fw.at[enc], recv_fw.at[enc], mate)
    copy.start()
    copies_d.append(copy)
    for to, where in other_encs():
        copy = remote(hidden.at[enc, mb], hidden.at[enc, mb], send_d.at[to], recv_d.at[enc], where)
        copy.start()
        copies_d.append(copy)

    for at, where in other_tps():
        remote(text_cols.at[at], text_cols.at[at], send_t.at[at], recv_t.at[at], where).wait_recv()
    tile = tiles(kv_cols, 256)

    @pl.loop(0, kv_cols // tile)
    def _(i):
        at = pl.ds(pl.multiple_of(i * tile, tile), tile)
        lhs = text_cols[...].reshape(n_tp * tokens, feats)
        out = jnp.dot(lhs, kv_w[:, at], preferred_element_type=F32)
        text_part[:, :, at] = out.astype(BF16).reshape(n_tp, tokens, tile)

    copies_u = []
    for to, where in other_tps():
        copy = remote(text_part.at[to], text_in.at[tp], send_u.at[to], recv_u.at[tp], where)
        copy.start()
        copies_u.append(copy)

    for at, where in other_encs():
        remote(hidden.at[at, mb], hidden.at[at, mb], send_d.at[at], recv_d.at[at], where).wait_recv()
        copy = remote(hidden.at[at, mb], hidden.at[at, mb], send_fw.at[at], recv_fw.at[at], mate)
        copy.start()
        copies_d.append(copy)
    for at in range(n_enc):
        remote(
            hidden.at[at, 1 - mb], hidden.at[at, 1 - mb], send_fw.at[at], recv_fw.at[at], mate
        ).wait_recv()

    local[1].wait()
    tile = tiles(cols, 256)

    @pl.loop(0, cols // tile)
    def _(i):
        at = pl.ds(pl.multiple_of(i * tile, tile), tile)
        lhs = hidden[...].reshape(groups * seq_rows, units)
        out = jnp.dot(lhs, down_w[:, at], preferred_element_type=F32)
        lowered[:, :, :, at] = out.astype(BF16).reshape(groups, n_tp, own, tile)

    copies_e = []
    for to, where in other_tps():
        copy = remote(lowered.at[:, to], low_in.at[tp], send_e.at[to], recv_e.at[tp], where)
        copy.start()
        copies_e.append(copy)
    for at, where in other_tps():
        remote(lowered.at[:, at], low_in.at[at], send_e.at[at], recv_e.at[at], where).wait_recv()
    low_in[tp] = lowered[:, tp]
    copies_f = []

    def finish(to):
        out = down_bias[...] + jnp.zeros((own, cols), F32)
        for t in range(n_tp):
            out = out + low_in[t, to].astype(F32)
        vis_part[to] = out.astype(BF16)

    for to, where in other_groups():
        finish(to)
        copy = remote(vis_part.at[to], visual.at[tp, me], send_f.at[to], recv_f.at[me], where)
        copy.start()
        copies_f.append(copy)
    finish(me)
    visual[tp, me] = vis_part[me]
    for at, where in other_groups():
        remote(vis_part.at[at], visual.at[tp, at], send_f.at[at], recv_f.at[at], where).wait_recv()
    copies_g = []
    for to, where in other_tps():
        copy = remote(visual.at[tp], visual.at[tp], send_g.at[to], recv_g.at[tp], where)
        copy.start()
        copies_g.append(copy)
    for at, where in other_tps():
        remote(visual.at[at], visual.at[at], send_g.at[at], recv_g.at[at], where).wait_recv()

    tile = tiles(kv_cols, 512)

    @pl.loop(0, kv_cols // tile)
    def _(i):
        at = pl.ds(pl.multiple_of(i * tile, tile), tile)
        out = jnp.zeros((seq_rows, tile), F32)
        for j in range(per_feat):
            lhs = visual[:, tp * per_feat + j].reshape(seq_rows, cols)
            out = out + jnp.dot(lhs, kv_w[j * cols : (j + 1) * cols, at], preferred_element_type=F32)
        vkv[:, :, at] = out.astype(BF16).reshape(n_tp, own, tile)

    copies_h = []
    for to, where in other_tps():
        copy = remote(vkv.at[to], vkv_in.at[tp], send_h.at[to], recv_h.at[tp], where)
        copy.start()
        copies_h.append(copy)
    vkv_in[tp] = vkv[tp]
    for at, where in other_tps():
        remote(vkv.at[at], vkv_in.at[at], send_h.at[at], recv_h.at[at], where).wait_recv()
    out = vkv_in[0].astype(F32)
    for t in range(1, n_tp):
        out = out + vkv_in[t].astype(F32)
    vkv_all[tp] = out.astype(BF16)
    copies_i = []
    for to, where in other_tps():
        copy = remote(vkv_all.at[tp], vkv_all.at[tp], send_i.at[to], recv_i.at[tp], where)
        copy.start()
        copies_i.append(copy)

    def place(i, squares):
        at = pl.ds(pl.multiple_of(i * cols, cols), cols)
        found = jnp.dot(
            picks[...], visual[:, i].reshape(seq_rows, cols), preferred_element_type=F32
        ).astype(BF16).astype(F32)
        mask = jnp.broadcast_to(present[...], (tokens, cols)) > 0
        values = jnp.where(mask, found, text[:, at].astype(F32))
        embedded[:, at] = values.astype(BF16)
        return squares + jnp.sum(values * values, axis=-1, keepdims=True)

    squares = lax.fori_loop(0, groups, place, jnp.zeros((tokens, 1), F32))
    scale = lax.rsqrt(squares * (1.0 / (groups * cols)) + 1e-06)

    text_in[tp] = text_part[tp]
    for at, where in other_tps():
        remote(text_part.at[at], text_in.at[at], send_u.at[at], recv_u.at[at], where).wait_recv()
    for at, where in other_tps():
        remote(vkv_all.at[at], vkv_all.at[at], send_i.at[at], recv_i.at[at], where).wait_recv()

    @pl.loop(0, kv_cols // tile)
    def _(i):
        at = pl.ds(pl.multiple_of(i * tile, tile), tile)
        found = jnp.dot(
            picks[...], vkv_all[:, :, at].reshape(seq_rows, tile), preferred_element_type=F32
        )
        plain = text_in[0, :, at].astype(F32)
        for t in range(1, n_tp):
            plain = plain + text_in[t, :, at].astype(F32)
        mask = jnp.broadcast_to(present[...], (tokens, tile)) > 0
        keys_values[:, at] = (jnp.where(mask, found, plain) * scale + kv_bias[:, at]).astype(BF16)

    to_pair.wait_send()
    for copies in (
        copies_a, copies_b, copies_t, copies_c, copies_d, copies_u,
        copies_e, copies_f, copies_g, copies_h, copies_i,
    ):
        for copy in copies:
            copy.wait_send()


def per_device(
    patches,
    patch_counts,
    dest_pos,
    merge_gain,
    merge_bias,
    up_weight,
    up_bias,
    down_weight,
    down_bias,
    text_embed,
    norm_gain,
    kv_weight,
    kv_bias,
):
    n_enc, n_tp = lax.axis_size("enc"), lax.axis_size("tp")
    groups = n_enc * lax.axis_size("mb")
    tp = lax.axis_index("tp")
    group = lax.axis_index("enc") * lax.axis_size("mb") + lax.axis_index("mb")
    text = text_embed[0, 0]
    tokens, width = text.shape
    feats, kv_cols = kv_weight.shape
    kw, units = up_weight.shape
    cols = down_weight.shape[1]
    own = patches.shape[2] // 4
    seq_rows = own * n_tp

    live_rows = patch_counts[0, 0] // 4
    live = (jnp.arange(SLOT, dtype=jnp.int32)[None, :] < live_rows[:, None]).reshape(-1)
    places = tp * tokens + jnp.arange(tokens, dtype=jnp.int32)
    select = (dest_pos[0, 0][None, :] == places[:, None]) & live[None, :]
    picks = select.astype(BF16)
    present = jnp.any(select, axis=1)[:, None].astype(jnp.int32)
    by_piece = patches[0, 0].reshape(own, 4, patches.shape[3]).transpose(1, 0, 2)

    dma = pltpu.SemaphoreType.DMA
    vmem = pl.BlockSpec(memory_space=pltpu.VMEM)
    hbm = pl.BlockSpec(memory_space=pl.ANY)
    by_group, by_enc, by_tp = [dma((groups,))] * 2, [dma((n_enc,))] * 2, [dma((n_tp,))] * 2
    embedded, keys_values = pl.pallas_call(
        functools.partial(kernel, (n_enc, n_tp)),
        out_shape=(
            jax.ShapeDtypeStruct((tokens, width), BF16),
            jax.ShapeDtypeStruct((tokens, kv_cols), BF16),
        ),
        in_specs=[vmem] * 9 + [hbm] * 4,
        out_specs=(vmem, vmem),
        scratch_shapes=[
            pltpu.VMEM((kw, units), BF16),
            pltpu.VMEM((units, cols), BF16),
            pltpu.VMEM((feats, kv_cols), BF16),
            pltpu.VMEM((tokens, width), BF16),
            pltpu.VMEM((groups, own, kw), BF16),
            pltpu.VMEM((groups, n_tp, own, kw), BF16),
            pltpu.VMEM((n_enc, 2, seq_rows, units), BF16),
            pltpu.VMEM((n_enc, seq_rows, units), BF16),
            pltpu.VMEM((n_enc, seq_rows, units), BF16),
            pltpu.VMEM((n_enc, seq_rows, units), BF16),
            pltpu.VMEM((n_enc, 2, seq_rows, units), BF16),
            pltpu.VMEM((groups, n_tp, own, cols), BF16),
            pltpu.VMEM((n_tp, groups, own, cols), BF16),
            pltpu.VMEM((groups, own, cols), BF16),
            pltpu.VMEM((n_tp, groups, own, cols), BF16),
            pltpu.VMEM((n_tp, own, kv_cols), BF16),
            pltpu.VMEM((n_tp, own, kv_cols), BF16),
            pltpu.VMEM((n_tp, own, kv_cols), BF16),
            pltpu.VMEM((n_tp, tokens, feats), BF16),
            pltpu.VMEM((n_tp, tokens, kv_cols), BF16),
            pltpu.VMEM((n_tp, tokens, kv_cols), BF16),
            dma((4,)),
        ]
        + by_group + by_tp + [dma, dma] + by_enc + by_enc + by_enc
        + by_tp + by_group + by_tp + by_tp + by_tp + by_tp + by_tp,
        compiler_params=pltpu.CompilerParams(
            collective_id=0, has_side_effects=True, vmem_limit_bytes=60 * 1024 * 1024
        ),
        cost_estimate=pl.CostEstimate(
            flops=2 * groups * seq_rows * units * (kw + cols) + 2 * n_tp * tokens * feats * kv_cols,
            bytes_accessed=2 * (kw * units + units * cols + feats * kv_cols + 2 * tokens * width),
            transcendentals=seq_rows * units,
        ),
    )(
        by_piece,
        merge_gain[None],
        merge_bias[None],
        lax.dynamic_slice_in_dim(up_bias, tp * units, units, 0)[None],
        lax.dynamic_slice_in_dim(down_bias, group * cols, cols, 0)[None],
        lax.dynamic_slice_in_dim(norm_gain, tp * feats, feats, 0)[:, None],
        kv_bias[None],
        picks,
        present,
        up_weight,
        down_weight,
        kv_weight,
        text,
    )
    return (embedded[None, None], keys_values[None, None])


def solution(mesh):
    return jax.shard_map(
        per_device,
        mesh=mesh,
        in_specs=(
            P("enc", "mb", "tp", None),
            P("enc", "mb", None),
            P("enc", "mb", None),
            P(),
            P(),
            P(("enc", "mb"), "tp"),
            P(),
            P("tp", ("enc", "mb")),
            P(),
            P("enc", "mb", "tp", None),
            P(),
            P("tp", None),
            P(),
        ),
        out_specs=(P("enc", "mb", "tp", None), P("enc", "mb", "tp", None)),
        check_vma=False,
    )
```

```python
import functools

import jax
import jax.numpy as jnp
from jax import lax
from jax.experimental import pallas as pl
from jax.experimental.pallas import tpu as pltpu
from jax.sharding import PartitionSpec as P

SLOT = 8
F32 = jnp.float32
BF16 = jnp.bfloat16
MESH = pl.DeviceIdType.MESH


def tiles(width, tile):
    return tile if width % tile == 0 else width


def kernel(
    dims,
    patches,
    params,
    dest,
    up_hbm,
    down_hbm,
    kv_hbm,
    text_hbm,
    embedded,
    keys_values,
    up_w,
    down_w,
    kv_w,
    text,
    split,
    rows,
    part,
    pair,
    chip_sum,
    summed,
    hidden,
    lowered,
    low_in,
    vis_part,
    visual,
    vkv,
    vkv_in,
    vkv_all,
    text_cols,
    text_part,
    text_in,
    picks,
    present,
    local_sem,
    send_a,
    recv_a,
    send_b,
    recv_b,
    send_pair,
    recv_pair,
    send_c,
    recv_c,
    send_d,
    recv_d,
    send_fw,
    recv_fw,
    send_e,
    recv_e,
    send_f,
    recv_f,
    send_g,
    recv_g,
    send_h,
    recv_h,
    send_i,
    recv_i,
    send_t,
    recv_t,
    send_u,
    recv_u,
):
    n_enc, n_tp = dims
    groups = 2 * n_enc
    enc, mb, tp = lax.axis_index("enc"), lax.axis_index("mb"), lax.axis_index("tp")
    me = enc * 2 + mb
    own, kw = split.shape[1], split.shape[2]
    width = patches.shape[1]
    units = up_w.shape[1]
    cols = down_w.shape[1]
    feats, kv_cols = kv_w.shape
    tokens = text.shape[0]
    seq_rows = n_tp * own
    per_feat = feats // cols
    cuts = [0]
    for size in (width, width, kv_cols, feats, cols, units):
        cuts.append(cuts[-1] + size)
    merge_gain, merge_bias, kv_bias, norm_gain, down_bias, up_bias = (
        params.at[:, start:stop] for start, stop in zip(cuts[:-1], cuts[1:])
    )

    def other_groups():
        for step in range(1, groups):
            to = lax.rem(me + step, groups)
            yield to, {"enc": lax.div(to, 2), "mb": lax.rem(to, 2)}

    def other_encs():
        for step in range(1, n_enc):
            to = lax.rem(enc + step, n_enc)
            yield to, {"enc": to}

    def other_tps():
        for step in range(1, n_tp):
            to = lax.rem(tp + step, n_tp)
            yield to, {"tp": to}

    mate = {"mb": 1 - mb}

    def remote(src, dst, send, recv, to):
        return pltpu.make_async_remote_copy(
            src_ref=src, dst_ref=dst, send_sem=send, recv_sem=recv, device_id=to, device_id_type=MESH
        )

    local = [
        pltpu.make_async_copy(src, dst, local_sem.at[i])
        for i, (src, dst) in enumerate(
            ((up_hbm, up_w), (down_hbm, down_w), (kv_hbm, kv_w), (text_hbm, text))
        )
    ]
    for copy in local:
        copy.start()

    barrier = pltpu.get_barrier_semaphore()
    for _, to in other_groups():
        pl.semaphore_signal(barrier, inc=1, device_id=to, device_id_type=MESH)
    for _, to in other_tps():
        pl.semaphore_signal(barrier, inc=1, device_id=to, device_id_type=MESH)

    values = patches[...].astype(F32)
    center = values - jnp.mean(values, axis=-1, keepdims=True)
    spread = jnp.mean(center * center, axis=-1, keepdims=True)
    normal = (center * lax.rsqrt(spread + 1e-06) * merge_gain[...] + merge_bias[...]).astype(BF16)
    row = lax.broadcasted_iota(jnp.int32, (own, 4 * own), 0)
    column = lax.broadcasted_iota(jnp.int32, (own, 4 * own), 1)
    for j in range(4):
        chosen = jnp.where(column == 4 * row + j, 1.0, 0.0).astype(BF16)
        every = jnp.dot(chosen, normal, preferred_element_type=F32).astype(BF16)
        for piece in range(width // kw):
            split[j * (width // kw) + piece] = every[:, piece * kw : (piece + 1) * kw]
    place_of = lax.broadcasted_iota(jnp.int32, (tokens, seq_rows), 0)
    chosen = jnp.where(place_of == dest[...], 1.0, 0.0)
    picks[...] = chosen.astype(BF16)
    present[...] = jnp.sum(chosen, axis=-1, keepdims=True)
    pl.semaphore_wait(barrier, groups - 1 + n_tp - 1)

    copies_a = []
    for to, where in other_groups():
        copy = remote(split.at[to], rows.at[enc, mb, tp], send_a.at[to], recv_a.at[me], where)
        copy.start()
        copies_a.append(copy)
    rows[enc, mb, tp] = split[me]
    for at, where in other_groups():
        remote(split.at[at], rows.at[lax.div(at, 2), lax.rem(at, 2), tp], send_a.at[at], recv_a.at[at], where).wait_recv()
    copies_b = []
    for to, where in other_tps():
        copy = remote(rows.at[:, :, tp], rows.at[:, :, tp], send_b.at[to], recv_b.at[tp], where)
        copy.start()
        copies_b.append(copy)

    local[0].wait()
    for at, where in other_tps():
        remote(rows.at[:, :, at], rows.at[:, :, at], send_b.at[at], recv_b.at[at], where).wait_recv()

    copies_t = []
    for to, where in other_tps():
        copy = remote(
            text_hbm.at[:, pl.ds(pl.multiple_of(to * feats, feats), feats)],
            text_cols.at[tp],
            send_t.at[to],
            recv_t.at[tp],
            where,
        )
        copy.start()
        copies_t.append(copy)

    tile = tiles(units, 256)

    def raise_half(half):
        @pl.loop(0, units // tile)
        def _(i):
            at = pl.ds(pl.multiple_of(i * tile, tile), tile)
            lhs = rows[:, half].reshape(n_enc * seq_rows, kw)
            out = jnp.dot(lhs, up_w[:, at], preferred_element_type=F32)
            part[:, half, :, at] = out.astype(BF16).reshape(n_enc, seq_rows, tile)

    raise_half(1 - mb)
    to_pair = remote(part.at[:, 1 - mb], pair, send_pair, recv_pair, mate)
    to_pair.start()
    raise_half(mb)
    to_pair.wait_recv()
    copies_c = []
    for to, where in other_encs():
        chip_sum[to] = (part[to, mb].astype(F32) + pair[to].astype(F32)).astype(BF16)
        copy = remote(chip_sum.at[to], summed.at[enc], send_c.at[to], recv_c.at[enc], where)
        copy.start()
        copies_c.append(copy)

    local[3].wait()
    text_cols[tp] = text[:, pl.ds(pl.multiple_of(tp * feats, feats), feats)]

    total = part[enc, mb].astype(F32) + pair[enc].astype(F32) + up_bias[...]
    for at, where in other_encs():
        remote(chip_sum.at[at], summed.at[at], send_c.at[at], recv_c.at[at], where).wait_recv()
        total = total + summed[at].astype(F32)
    hidden[enc, mb] = (0.5 * total * (1.0 + lax.erf(total * 0.7071067811865476))).astype(BF16)

    copies_d = []
    copy = remote(hidden.at[enc, mb], hidden.at[enc, mb], send_fw.at[enc], recv_fw.at[enc], mate)
    copy.start()
    copies_d.append(copy)
    for to, where in other_encs():
        copy = remote(hidden.at[enc, mb], hidden.at[enc, mb], send_d.at[to], recv_d.at[enc], where)
        copy.start()
        copies_d.append(copy)

    for at, where in other_tps():
        remote(text_cols.at[at], text_cols.at[at], send_t.at[at], recv_t.at[at], where).wait_recv()
    local[2].wait()
    for at in range(n_tp):
        text_cols[at] = (text_cols[at].astype(F32) * norm_gain[...]).astype(BF16)
    tile = tiles(kv_cols, 256)

    @pl.loop(0, kv_cols // tile)
    def _(i):
        at = pl.ds(pl.multiple_of(i * tile, tile), tile)
        lhs = text_cols[...].reshape(n_tp * tokens, feats)
        out = jnp.dot(lhs, kv_w[:, at], preferred_element_type=F32)
        text_part[:, :, at] = out.astype(BF16).reshape(n_tp, tokens, tile)

    half = kv_cols // 2

    def text_piece(h, src, dst, to, where):
        at = pl.ds(h * half, half)
        return remote(
            text_part.at[src, :, at], text_in.at[dst, :, at], send_u.at[h, to], recv_u.at[h, dst], where
        )

    copies_u = []

    def send_text(h):
        for to, where in other_tps():
            copy = text_piece(h, to, tp, to, where)
            copy.start()
            copies_u.append(copy)

    send_text(0)

    for at, where in other_encs():
        remote(hidden.at[at, mb], hidden.at[at, mb], send_d.at[at], recv_d.at[at], where).wait_recv()
        copy = remote(hidden.at[at, mb], hidden.at[at, mb], send_fw.at[at], recv_fw.at[at], mate)
        copy.start()
        copies_d.append(copy)
    for at in range(n_enc):
        remote(
            hidden.at[at, 1 - mb], hidden.at[at, 1 - mb], send_fw.at[at], recv_fw.at[at], mate
        ).wait_recv()

    local[1].wait()
    tile = tiles(cols, 256)

    @pl.loop(0, cols // tile)
    def _(i):
        at = pl.ds(pl.multiple_of(i * tile, tile), tile)
        lhs = hidden[...].reshape(groups * seq_rows, units)
        out = jnp.dot(lhs, down_w[:, at], preferred_element_type=F32)
        lowered[:, :, :, at] = out.astype(BF16).reshape(groups, n_tp, own, tile)

    copies_e = []
    for to, where in other_tps():
        copy = remote(lowered.at[:, to], low_in.at[tp], send_e.at[to], recv_e.at[tp], where)
        copy.start()
        copies_e.append(copy)
    for at, where in other_tps():
        remote(lowered.at[:, at], low_in.at[at], send_e.at[at], recv_e.at[at], where).wait_recv()
    send_text(1)
    low_in[tp] = lowered[:, tp]
    copies_f = []

    def finish(to):
        out = down_bias[...] + jnp.zeros((own, cols), F32)
        for t in range(n_tp):
            out = out + low_in[t, to].astype(F32)
        vis_part[to] = out.astype(BF16)

    for to, where in other_groups():
        finish(to)
        copy = remote(vis_part.at[to], visual.at[tp, me], send_f.at[to], recv_f.at[me], where)
        copy.start()
        copies_f.append(copy)
    finish(me)
    visual[tp, me] = vis_part[me]
    for at, where in other_groups():
        remote(vis_part.at[at], visual.at[tp, at], send_f.at[at], recv_f.at[at], where).wait_recv()

    def visual_piece(of, block, to, where):
        at = visual.at[of, pl.ds(block * per_feat, per_feat)]
        return remote(at, at, send_g.at[to, block], recv_g.at[of, block], where)

    for to, where in other_tps():
        visual_piece(tp, to, to, where).start()
    for at, where in other_tps():
        visual_piece(at, tp, at, where).wait_recv()
    for to, where in other_tps():

        @pl.loop(1, n_tp)
        def _(step):
            visual_piece(tp, lax.rem(to + step, n_tp), to, where).start()

    tile = tiles(kv_cols, 512)

    @pl.loop(0, kv_cols // tile)
    def _(i):
        at = pl.ds(pl.multiple_of(i * tile, tile), tile)
        out = jnp.zeros((seq_rows, tile), F32)
        for j in range(per_feat):
            gain = norm_gain[:, j * cols : (j + 1) * cols]
            lhs = visual[:, tp * per_feat + j].reshape(seq_rows, cols)
            lhs = (lhs.astype(F32) * gain).astype(BF16)
            out = out + jnp.dot(lhs, kv_w[j * cols : (j + 1) * cols, at], preferred_element_type=F32)
        vkv[:, :, at] = out.astype(BF16).reshape(n_tp, own, tile)

    copies_h = []
    for to, where in other_tps():
        copy = remote(vkv.at[to], vkv_in.at[tp], send_h.at[to], recv_h.at[tp], where)
        copy.start()
        copies_h.append(copy)
    vkv_in[tp] = vkv[tp]
    for at, where in other_tps():
        remote(vkv.at[at], vkv_in.at[at], send_h.at[at], recv_h.at[at], where).wait_recv()
    out = vkv_in[0].astype(F32)
    for t in range(1, n_tp):
        out = out + vkv_in[t].astype(F32)
    vkv_all[tp] = out.astype(BF16)
    copies_i = []
    for to, where in other_tps():
        copy = remote(vkv_all.at[tp], vkv_all.at[tp], send_i.at[to], recv_i.at[tp], where)
        copy.start()
        copies_i.append(copy)

    for at, where in other_tps():

        @pl.loop(1, n_tp)
        def _(step):
            visual_piece(at, lax.rem(tp + step, n_tp), at, where).wait_recv()

    def place(i, squares):
        at = pl.ds(pl.multiple_of(i * cols, cols), cols)
        found = jnp.dot(
            picks[...], visual[:, i].reshape(seq_rows, cols), preferred_element_type=F32
        ).astype(BF16).astype(F32)
        mask = jnp.broadcast_to(present[...], (tokens, cols)) > 0.5
        values = jnp.where(mask, found, text[:, at].astype(F32))
        embedded[:, at] = values.astype(BF16)
        return squares + jnp.sum(values * values, axis=-1, keepdims=True)

    squares = lax.fori_loop(0, groups, place, jnp.zeros((tokens, 1), F32))
    scale = lax.rsqrt(squares * (1.0 / (groups * cols)) + 1e-06)

    text_in[tp] = text_part[tp]
    for at, where in other_tps():
        for h in range(2):
            text_piece(h, at, at, at, where).wait_recv()
    for at, where in other_tps():
        remote(vkv_all.at[at], vkv_all.at[at], send_i.at[at], recv_i.at[at], where).wait_recv()

    @pl.loop(0, kv_cols // tile)
    def _(i):
        at = pl.ds(pl.multiple_of(i * tile, tile), tile)
        found = jnp.dot(
            picks[...], vkv_all[:, :, at].reshape(seq_rows, tile), preferred_element_type=F32
        )
        plain = text_in[0, :, at].astype(F32)
        for t in range(1, n_tp):
            plain = plain + text_in[t, :, at].astype(F32)
        mask = jnp.broadcast_to(present[...], (tokens, tile)) > 0.5
        keys_values[:, at] = (jnp.where(mask, found, plain) * scale + kv_bias[:, at]).astype(BF16)

    to_pair.wait_send()
    for copies in (
        copies_a, copies_b, copies_t, copies_c, copies_d, copies_u,
        copies_e, copies_f, copies_h, copies_i,
    ):
        for copy in copies:
            copy.wait_send()
    for to, where in other_tps():

        @pl.loop(0, n_tp)
        def _(block):
            visual_piece(tp, block, to, where).wait_send()


def per_device(
    patches,
    patch_counts,
    dest_pos,
    merge_gain,
    merge_bias,
    up_weight,
    up_bias,
    down_weight,
    down_bias,
    text_embed,
    norm_gain,
    kv_weight,
    kv_bias,
):
    n_enc, n_tp = lax.axis_size("enc"), lax.axis_size("tp")
    groups = n_enc * lax.axis_size("mb")
    tp = lax.axis_index("tp")
    group = lax.axis_index("enc") * lax.axis_size("mb") + lax.axis_index("mb")
    text = text_embed[0, 0]
    tokens, width = text.shape
    feats, kv_cols = kv_weight.shape
    kw, units = up_weight.shape
    cols = down_weight.shape[1]
    own = patches.shape[2] // 4
    seq_rows = own * n_tp

    live_rows = patch_counts[0, 0] // 4
    live = (jnp.arange(SLOT, dtype=jnp.int32)[None, :] < live_rows[:, None]).reshape(-1)
    dest = (jnp.where(live, dest_pos[0, 0], -1) - tp * tokens)[None]
    params = jnp.concatenate(
        [
            merge_gain,
            merge_bias,
            kv_bias,
            lax.dynamic_slice_in_dim(norm_gain, tp * feats, feats, 0),
            lax.dynamic_slice_in_dim(down_bias, group * cols, cols, 0),
            lax.dynamic_slice_in_dim(up_bias, tp * units, units, 0),
        ]
    )[None]

    dma = pltpu.SemaphoreType.DMA
    vmem = pl.BlockSpec(memory_space=pltpu.VMEM)
    hbm = pl.BlockSpec(memory_space=pl.ANY)
    by_group, by_enc, by_tp = [dma((groups,))] * 2, [dma((n_enc,))] * 2, [dma((n_tp,))] * 2
    embedded, keys_values = pl.pallas_call(
        functools.partial(kernel, (n_enc, n_tp)),
        out_shape=(
            jax.ShapeDtypeStruct((tokens, width), BF16),
            jax.ShapeDtypeStruct((tokens, kv_cols), BF16),
        ),
        in_specs=[vmem] * 3 + [hbm] * 4,
        out_specs=(vmem, vmem),
        scratch_shapes=[
            pltpu.VMEM((kw, units), BF16),
            pltpu.VMEM((units, cols), BF16),
            pltpu.VMEM((feats, kv_cols), BF16),
            pltpu.VMEM((tokens, width), BF16),
            pltpu.VMEM((groups, own, kw), BF16),
            pltpu.VMEM((n_enc, 2, n_tp, own, kw), BF16),
            pltpu.VMEM((n_enc, 2, seq_rows, units), BF16),
            pltpu.VMEM((n_enc, seq_rows, units), BF16),
            pltpu.VMEM((n_enc, seq_rows, units), BF16),
            pltpu.VMEM((n_enc, seq_rows, units), BF16),
            pltpu.VMEM((n_enc, 2, seq_rows, units), BF16),
            pltpu.VMEM((groups, n_tp, own, cols), BF16),
            pltpu.VMEM((n_tp, groups, own, cols), BF16),
            pltpu.VMEM((groups, own, cols), BF16),
            pltpu.VMEM((n_tp, groups, own, cols), BF16),
            pltpu.VMEM((n_tp, own, kv_cols), BF16),
            pltpu.VMEM((n_tp, own, kv_cols), BF16),
            pltpu.VMEM((n_tp, own, kv_cols), BF16),
            pltpu.VMEM((n_tp, tokens, feats), BF16),
            pltpu.VMEM((n_tp, tokens, kv_cols), BF16),
            pltpu.VMEM((n_tp, tokens, kv_cols), BF16),
            pltpu.VMEM((tokens, seq_rows), BF16),
            pltpu.VMEM((tokens, 1), F32),
            dma((4,)),
        ]
        + by_group + by_tp + [dma, dma] + by_enc + by_enc + by_enc
        + by_tp + by_group + [dma((n_tp, n_tp))] * 2 + by_tp + by_tp + by_tp + [dma((2, n_tp))] * 2,
        compiler_params=pltpu.CompilerParams(
            collective_id=0, has_side_effects=True, vmem_limit_bytes=60 * 1024 * 1024
        ),
        cost_estimate=pl.CostEstimate(
            flops=2 * groups * seq_rows * units * (kw + cols) + 2 * n_tp * tokens * feats * kv_cols,
            bytes_accessed=2 * (kw * units + units * cols + feats * kv_cols + 2 * tokens * width),
            transcendentals=seq_rows * units,
        ),
    )(
        patches[0, 0],
        params,
        dest,
        up_weight,
        down_weight,
        kv_weight,
        text,
    )
    return (embedded[None, None], keys_values[None, None])


def solution(mesh):
    return jax.shard_map(
        per_device,
        mesh=mesh,
        in_specs=(
            P("enc", "mb", "tp", None),
            P("enc", "mb", None),
            P("enc", "mb", None),
            P(),
            P(),
            P(("enc", "mb"), "tp"),
            P(),
            P("tp", ("enc", "mb")),
            P(),
            P("enc", "mb", "tp", None),
            P(),
            P("tp", None),
            P(),
        ),
        out_specs=(P("enc", "mb", "tp", None), P("enc", "mb", "tp", None)),
        check_vma=False,
    )
```

```python
import functools

import jax
import jax.numpy as jnp
from jax import lax
from jax.experimental import pallas as pl
from jax.experimental.pallas import tpu as pltpu
from jax.sharding import PartitionSpec as P

SLOT = 8
F32 = jnp.float32
BF16 = jnp.bfloat16
MESH = pl.DeviceIdType.MESH


def tiles(width, tile):
    return tile if width % tile == 0 else width


def kernel(
    dims,
    patches,
    params,
    dest,
    up_hbm,
    down_hbm,
    kv_hbm,
    text_hbm,
    embedded,
    keys_values,
    up_w,
    down_w,
    kv_w,
    text,
    split,
    rows,
    part,
    pair,
    chip_sum,
    summed,
    hidden,
    lowered,
    low_in,
    vis_part,
    visual,
    vkv,
    vkv_in,
    vkv_all,
    text_cols,
    text_part,
    text_in,
    picks,
    present,
    local_sem,
    send_a,
    recv_a,
    send_b,
    recv_b,
    send_pair,
    recv_pair,
    send_c,
    recv_c,
    send_d,
    recv_d,
    send_fw,
    recv_fw,
    send_e,
    recv_e,
    send_f,
    recv_f,
    send_g,
    recv_g,
    send_h,
    recv_h,
    send_i,
    recv_i,
    send_t,
    recv_t,
    send_u,
    recv_u,
):
    n_enc, n_tp = dims
    groups = 2 * n_enc
    enc, mb, tp = lax.axis_index("enc"), lax.axis_index("mb"), lax.axis_index("tp")
    me = enc * 2 + mb
    own, kw = split.shape[1], split.shape[2]
    width = patches.shape[1]
    units = up_w.shape[1]
    cols = down_w.shape[1]
    feats, kv_cols = kv_w.shape
    tokens = text.shape[0]
    seq_rows = n_tp * own
    per_feat = feats // cols
    cuts = [0]
    for size in (width, width, kv_cols, feats, cols, units):
        cuts.append(cuts[-1] + size)
    merge_gain, merge_bias, kv_bias, norm_gain, down_bias, up_bias = (
        params.at[:, start:stop] for start, stop in zip(cuts[:-1], cuts[1:])
    )

    def other_groups():
        for step in range(1, groups):
            to = lax.rem(me + step, groups)
            yield to, {"enc": lax.div(to, 2), "mb": lax.rem(to, 2)}

    def other_encs():
        for step in range(1, n_enc):
            to = lax.rem(enc + step, n_enc)
            yield to, {"enc": to}

    def other_tps():
        for step in range(1, n_tp):
            to = lax.rem(tp + step, n_tp)
            yield to, {"tp": to}

    mate = {"mb": 1 - mb}

    def remote(src, dst, send, recv, to):
        return pltpu.make_async_remote_copy(
            src_ref=src, dst_ref=dst, send_sem=send, recv_sem=recv, device_id=to, device_id_type=MESH
        )

    local = [
        pltpu.make_async_copy(src, dst, local_sem.at[i])
        for i, (src, dst) in enumerate(
            ((up_hbm, up_w), (down_hbm, down_w), (kv_hbm, kv_w), (text_hbm, text))
        )
    ]
    for copy in local:
        copy.start()

    barrier = pltpu.get_barrier_semaphore()
    for _, to in other_groups():
        pl.semaphore_signal(barrier, inc=1, device_id=to, device_id_type=MESH)
    for _, to in other_tps():
        pl.semaphore_signal(barrier, inc=1, device_id=to, device_id_type=MESH)

    values = patches[...].astype(F32)
    center = values - jnp.mean(values, axis=-1, keepdims=True)
    spread = jnp.mean(center * center, axis=-1, keepdims=True)
    normal = (center * lax.rsqrt(spread + 1e-06) * merge_gain[...] + merge_bias[...]).astype(BF16)
    row = lax.broadcasted_iota(jnp.int32, (own, 4 * own), 0)
    column = lax.broadcasted_iota(jnp.int32, (own, 4 * own), 1)
    for j in range(4):
        chosen = jnp.where(column == 4 * row + j, 1.0, 0.0).astype(BF16)
        every = jnp.dot(chosen, normal, preferred_element_type=F32).astype(BF16)
        for piece in range(width // kw):
            split[j * (width // kw) + piece] = every[:, piece * kw : (piece + 1) * kw]
    place_of = lax.broadcasted_iota(jnp.int32, (tokens, seq_rows), 0)
    chosen = jnp.where(place_of == dest[...], 1.0, 0.0)
    picks[...] = chosen.astype(BF16)
    present[...] = jnp.sum(chosen, axis=-1, keepdims=True)
    pl.semaphore_wait(barrier, groups - 1 + n_tp - 1)

    quarter, half = tokens // 4, tokens // 2
    copies_t, copies_u = [], []

    def text_columns(q, of, to, where):
        at = pl.ds(q * quarter, quarter)
        return remote(
            text_hbm.at[at, pl.ds(pl.multiple_of(to * feats, feats), feats)],
            text_cols.at[of, at],
            send_t.at[q, to],
            recv_t.at[q, of],
            where,
        )

    def send_columns(q):
        for to, where in other_tps():
            copy = text_columns(q, tp, to, where)
            copy.start()
            copies_t.append(copy)

    def text_piece(h, src, dst, to, where):
        at = pl.ds(h * half, half)
        return remote(
            text_part.at[src, at], text_in.at[dst, at], send_u.at[h, to], recv_u.at[h, dst], where
        )

    def text_half(h):
        for q in (2 * h, 2 * h + 1):
            for at, where in other_tps():
                text_columns(q, at, at, where).wait_recv()
        span = slice(h * half, (h + 1) * half)
        for at in range(n_tp):
            text_cols[at, span] = (text_cols[at, span].astype(F32) * norm_gain[...]).astype(BF16)
        tile = tiles(kv_cols, 256)

        @pl.loop(0, kv_cols // tile)
        def _(i):
            at = pl.ds(pl.multiple_of(i * tile, tile), tile)
            lhs = text_cols[:, span].reshape(n_tp * half, feats)
            out = jnp.dot(lhs, kv_w[:, at], preferred_element_type=F32)
            text_part[:, span, at] = out.astype(BF16).reshape(n_tp, half, tile)

        for to, where in other_tps():
            copy = text_piece(h, to, tp, to, where)
            copy.start()
            copies_u.append(copy)

    copies_a = []
    for to, where in other_groups():
        copy = remote(split.at[to], rows.at[enc, mb, tp], send_a.at[to], recv_a.at[me], where)
        copy.start()
        copies_a.append(copy)
    send_columns(0)
    rows[enc, mb, tp] = split[me]
    for at, where in other_groups():
        remote(split.at[at], rows.at[lax.div(at, 2), lax.rem(at, 2), tp], send_a.at[at], recv_a.at[at], where).wait_recv()
    copies_b = []
    for to, where in other_tps():
        copy = remote(rows.at[:, :, tp], rows.at[:, :, tp], send_b.at[to], recv_b.at[tp], where)
        copy.start()
        copies_b.append(copy)

    local[0].wait()
    for at, where in other_tps():
        remote(rows.at[:, :, at], rows.at[:, :, at], send_b.at[at], recv_b.at[at], where).wait_recv()

    tile = tiles(units, 256)

    def raise_half(half):
        @pl.loop(0, units // tile)
        def _(i):
            at = pl.ds(pl.multiple_of(i * tile, tile), tile)
            lhs = rows[:, half].reshape(n_enc * seq_rows, kw)
            out = jnp.dot(lhs, up_w[:, at], preferred_element_type=F32)
            part[:, half, :, at] = out.astype(BF16).reshape(n_enc, seq_rows, tile)

    send_columns(1)
    raise_half(1 - mb)
    to_pair = remote(part.at[:, 1 - mb], pair, send_pair, recv_pair, mate)
    to_pair.start()
    raise_half(mb)
    to_pair.wait_recv()
    copies_c = []
    for to, where in other_encs():
        chip_sum[to] = (part[to, mb].astype(F32) + pair[to].astype(F32)).astype(BF16)
        copy = remote(chip_sum.at[to], summed.at[enc], send_c.at[to], recv_c.at[enc], where)
        copy.start()
        copies_c.append(copy)

    send_columns(2)
    send_columns(3)
    local[2].wait()
    local[3].wait()
    text_cols[tp] = text[:, pl.ds(pl.multiple_of(tp * feats, feats), feats)]

    text_half(0)

    total = part[enc, mb].astype(F32) + pair[enc].astype(F32) + up_bias[...]
    for at, where in other_encs():
        remote(chip_sum.at[at], summed.at[at], send_c.at[at], recv_c.at[at], where).wait_recv()
        total = total + summed[at].astype(F32)
    hidden[enc, mb] = (0.5 * total * (1.0 + lax.erf(total * 0.7071067811865476))).astype(BF16)

    copies_d = []
    copy = remote(hidden.at[enc, mb], hidden.at[enc, mb], send_fw.at[enc], recv_fw.at[enc], mate)
    copy.start()
    copies_d.append(copy)
    for to, where in other_encs():
        copy = remote(hidden.at[enc, mb], hidden.at[enc, mb], send_d.at[to], recv_d.at[enc], where)
        copy.start()
        copies_d.append(copy)

    text_half(1)
    for at, where in other_encs():
        remote(hidden.at[at, mb], hidden.at[at, mb], send_d.at[at], recv_d.at[at], where).wait_recv()
        copy = remote(hidden.at[at, mb], hidden.at[at, mb], send_fw.at[at], recv_fw.at[at], mate)
        copy.start()
        copies_d.append(copy)
    for at in range(n_enc):
        remote(
            hidden.at[at, 1 - mb], hidden.at[at, 1 - mb], send_fw.at[at], recv_fw.at[at], mate
        ).wait_recv()

    local[1].wait()
    wide = cols // 2
    copies_e, copies_f = [], []

    def sums_piece(h, to, dst, where):
        at = pl.ds(h * wide, wide)
        return remote(
            lowered.at[:, to, :, at], low_in.at[dst, :, :, at], send_e.at[h, to], recv_e.at[h, dst], where
        )

    for h in range(2):
        at = pl.ds(h * wide, wide)
        lhs = hidden[...].reshape(groups * seq_rows, units)
        out = jnp.dot(lhs, down_w[:, at], preferred_element_type=F32)
        lowered[:, :, :, at] = out.astype(BF16).reshape(groups, n_tp, own, wide)
        for to, where in other_tps():
            copy = sums_piece(h, to, tp, where)
            copy.start()
            copies_e.append(copy)
    low_in[tp] = lowered[:, tp]

    def rows_piece(h, to, of, where):
        at = pl.ds(h * wide, wide)
        return remote(
            vis_part.at[to, :, at], visual.at[tp, of, :, at], send_f.at[h, to], recv_f.at[h, of], where
        )

    for h in range(2):
        at = pl.ds(h * wide, wide)
        for of, where in other_tps():
            sums_piece(h, of, of, where).wait_recv()
        out = low_in[0, :, :, at].astype(F32)
        for t in range(1, n_tp):
            out = out + low_in[t, :, :, at].astype(F32)
        vis_part[:, :, at] = (out + down_bias[:, at]).astype(BF16)
        for to, where in other_groups():
            copy = rows_piece(h, to, me, where)
            copy.start()
            copies_f.append(copy)
    visual[tp, me] = vis_part[me]
    for h in range(2):
        for of, where in other_groups():
            rows_piece(h, of, of, where).wait_recv()

    def visual_piece(of, block, to, where):
        at = visual.at[of, pl.ds(block * per_feat, per_feat)]
        return remote(at, at, send_g.at[to, block], recv_g.at[of, block], where)

    for to, where in other_tps():
        visual_piece(tp, to, to, where).start()
    for at, where in other_tps():
        visual_piece(at, tp, at, where).wait_recv()
    for to, where in other_tps():

        @pl.loop(1, n_tp)
        def _(step):
            visual_piece(tp, lax.rem(to + step, n_tp), to, where).start()

    tile = tiles(kv_cols, 512)

    @pl.loop(0, kv_cols // tile)
    def _(i):
        at = pl.ds(pl.multiple_of(i * tile, tile), tile)
        out = jnp.zeros((seq_rows, tile), F32)
        for j in range(per_feat):
            gain = norm_gain[:, j * cols : (j + 1) * cols]
            lhs = visual[:, tp * per_feat + j].reshape(seq_rows, cols)
            lhs = (lhs.astype(F32) * gain).astype(BF16)
            out = out + jnp.dot(lhs, kv_w[j * cols : (j + 1) * cols, at], preferred_element_type=F32)
        vkv[:, :, at] = out.astype(BF16).reshape(n_tp, own, tile)

    copies_h = []
    for to, where in other_tps():
        copy = remote(vkv.at[to], vkv_in.at[tp], send_h.at[to], recv_h.at[tp], where)
        copy.start()
        copies_h.append(copy)
    vkv_in[tp] = vkv[tp]
    for at, where in other_tps():
        remote(vkv.at[at], vkv_in.at[at], send_h.at[at], recv_h.at[at], where).wait_recv()
    out = vkv_in[0].astype(F32)
    for t in range(1, n_tp):
        out = out + vkv_in[t].astype(F32)
    vkv_all[tp] = out.astype(BF16)
    copies_i = []
    for to, where in other_tps():
        copy = remote(vkv_all.at[tp], vkv_all.at[tp], send_i.at[to], recv_i.at[tp], where)
        copy.start()
        copies_i.append(copy)

    for at, where in other_tps():

        @pl.loop(1, n_tp)
        def _(step):
            visual_piece(at, lax.rem(tp + step, n_tp), at, where).wait_recv()

    def place(i, squares):
        at = pl.ds(pl.multiple_of(i * cols, cols), cols)
        found = jnp.dot(
            picks[...], visual[:, i].reshape(seq_rows, cols), preferred_element_type=F32
        ).astype(BF16).astype(F32)
        mask = jnp.broadcast_to(present[...], (tokens, cols)) > 0.5
        values = jnp.where(mask, found, text[:, at].astype(F32))
        embedded[:, at] = values.astype(BF16)
        return squares + jnp.sum(values * values, axis=-1, keepdims=True)

    squares = lax.fori_loop(0, groups, place, jnp.zeros((tokens, 1), F32))
    scale = lax.rsqrt(squares * (1.0 / (groups * cols)) + 1e-06)

    text_in[tp] = text_part[tp]
    for at, where in other_tps():
        for h in range(2):
            text_piece(h, at, at, at, where).wait_recv()
    for at, where in other_tps():
        remote(vkv_all.at[at], vkv_all.at[at], send_i.at[at], recv_i.at[at], where).wait_recv()

    @pl.loop(0, kv_cols // tile)
    def _(i):
        at = pl.ds(pl.multiple_of(i * tile, tile), tile)
        found = jnp.dot(
            picks[...], vkv_all[:, :, at].reshape(seq_rows, tile), preferred_element_type=F32
        )
        plain = text_in[0, :, at].astype(F32)
        for t in range(1, n_tp):
            plain = plain + text_in[t, :, at].astype(F32)
        mask = jnp.broadcast_to(present[...], (tokens, tile)) > 0.5
        keys_values[:, at] = (jnp.where(mask, found, plain) * scale + kv_bias[:, at]).astype(BF16)

    to_pair.wait_send()
    for copies in (
        copies_a, copies_b, copies_t, copies_c, copies_d, copies_u,
        copies_e, copies_f, copies_h, copies_i,
    ):
        for copy in copies:
            copy.wait_send()
    for to, where in other_tps():

        @pl.loop(0, n_tp)
        def _(block):
            visual_piece(tp, block, to, where).wait_send()


def per_device(
    patches,
    patch_counts,
    dest_pos,
    merge_gain,
    merge_bias,
    up_weight,
    up_bias,
    down_weight,
    down_bias,
    text_embed,
    norm_gain,
    kv_weight,
    kv_bias,
):
    n_enc, n_tp = lax.axis_size("enc"), lax.axis_size("tp")
    groups = n_enc * lax.axis_size("mb")
    tp = lax.axis_index("tp")
    group = lax.axis_index("enc") * lax.axis_size("mb") + lax.axis_index("mb")
    text = text_embed[0, 0]
    tokens, width = text.shape
    feats, kv_cols = kv_weight.shape
    kw, units = up_weight.shape
    cols = down_weight.shape[1]
    own = patches.shape[2] // 4
    seq_rows = own * n_tp

    live_rows = patch_counts[0, 0] // 4
    live = (jnp.arange(SLOT, dtype=jnp.int32)[None, :] < live_rows[:, None]).reshape(-1)
    dest = (jnp.where(live, dest_pos[0, 0], -1) - tp * tokens)[None]
    params = jnp.concatenate(
        [
            merge_gain,
            merge_bias,
            kv_bias,
            lax.dynamic_slice_in_dim(norm_gain, tp * feats, feats, 0),
            lax.dynamic_slice_in_dim(down_bias, group * cols, cols, 0),
            lax.dynamic_slice_in_dim(up_bias, tp * units, units, 0),
        ]
    )[None]

    dma = pltpu.SemaphoreType.DMA
    vmem = pl.BlockSpec(memory_space=pltpu.VMEM)
    hbm = pl.BlockSpec(memory_space=pl.ANY)
    by_group, by_enc, by_tp = [dma((groups,))] * 2, [dma((n_enc,))] * 2, [dma((n_tp,))] * 2
    embedded, keys_values = pl.pallas_call(
        functools.partial(kernel, (n_enc, n_tp)),
        out_shape=(
            jax.ShapeDtypeStruct((tokens, width), BF16),
            jax.ShapeDtypeStruct((tokens, kv_cols), BF16),
        ),
        in_specs=[vmem] * 3 + [hbm] * 4,
        out_specs=(vmem, vmem),
        scratch_shapes=[
            pltpu.VMEM((kw, units), BF16),
            pltpu.VMEM((units, cols), BF16),
            pltpu.VMEM((feats, kv_cols), BF16),
            pltpu.VMEM((tokens, width), BF16),
            pltpu.VMEM((groups, own, kw), BF16),
            pltpu.VMEM((n_enc, 2, n_tp, own, kw), BF16),
            pltpu.VMEM((n_enc, 2, seq_rows, units), BF16),
            pltpu.VMEM((n_enc, seq_rows, units), BF16),
            pltpu.VMEM((n_enc, seq_rows, units), BF16),
            pltpu.VMEM((n_enc, seq_rows, units), BF16),
            pltpu.VMEM((n_enc, 2, seq_rows, units), BF16),
            pltpu.VMEM((groups, n_tp, own, cols), BF16),
            pltpu.VMEM((n_tp, groups, own, cols), BF16),
            pltpu.VMEM((groups, own, cols), BF16),
            pltpu.VMEM((n_tp, groups, own, cols), BF16),
            pltpu.VMEM((n_tp, own, kv_cols), BF16),
            pltpu.VMEM((n_tp, own, kv_cols), BF16),
            pltpu.VMEM((n_tp, own, kv_cols), BF16),
            pltpu.VMEM((n_tp, tokens, feats), BF16),
            pltpu.VMEM((n_tp, tokens, kv_cols), BF16),
            pltpu.VMEM((n_tp, tokens, kv_cols), BF16),
            pltpu.VMEM((tokens, seq_rows), BF16),
            pltpu.VMEM((tokens, 1), F32),
            dma((4,)),
        ]
        + by_group + by_tp + [dma, dma] + by_enc + by_enc + by_enc
        + [dma((2, n_tp))] * 2 + [dma((2, groups))] * 2 + [dma((n_tp, n_tp))] * 2 + by_tp + by_tp
        + [dma((4, n_tp))] * 2 + [dma((2, n_tp))] * 2,
        compiler_params=pltpu.CompilerParams(
            collective_id=0, has_side_effects=True, vmem_limit_bytes=60 * 1024 * 1024
        ),
        cost_estimate=pl.CostEstimate(
            flops=2 * groups * seq_rows * units * (kw + cols) + 2 * n_tp * tokens * feats * kv_cols,
            bytes_accessed=2 * (kw * units + units * cols + feats * kv_cols + 2 * tokens * width),
            transcendentals=seq_rows * units,
        ),
    )(
        patches[0, 0],
        params,
        dest,
        up_weight,
        down_weight,
        kv_weight,
        text,
    )
    return (embedded[None, None], keys_values[None, None])


def solution(mesh):
    return jax.shard_map(
        per_device,
        mesh=mesh,
        in_specs=(
            P("enc", "mb", "tp", None),
            P("enc", "mb", None),
            P("enc", "mb", None),
            P(),
            P(),
            P(("enc", "mb"), "tp"),
            P(),
            P("tp", ("enc", "mb")),
            P(),
            P("enc", "mb", "tp", None),
            P(),
            P("tp", None),
            P(),
        ),
        out_specs=(P("enc", "mb", "tp", None), P("enc", "mb", "tp", None)),
        check_vma=False,
    )
```

```python
import functools

import jax
import jax.numpy as jnp
from jax import lax
from jax.experimental import pallas as pl
from jax.experimental.pallas import tpu as pltpu
from jax.sharding import PartitionSpec as P

SLOT = 8
F32 = jnp.float32
BF16 = jnp.bfloat16
MESH = pl.DeviceIdType.MESH


def tiles(width, tile):
    return tile if width % tile == 0 else width


def kernel(
    dims,
    patches,
    gain_in,
    bias_in,
    kv_bias_in,
    norm_gain_in,
    down_bias_in,
    up_bias_in,
    dest,
    up_hbm,
    down_hbm,
    kv_hbm,
    text_hbm,
    embedded,
    keys_values,
    up_w,
    down_w,
    kv_w,
    text,
    split,
    rows,
    part,
    pair,
    chip_sum,
    summed,
    hidden,
    lowered,
    low_in,
    vis_part,
    visual,
    vkv,
    vkv_in,
    vkv_all,
    text_cols,
    text_part,
    text_in,
    picks,
    present,
    params,
    local_sem,
    send_a,
    recv_a,
    send_b,
    recv_b,
    send_pair,
    recv_pair,
    send_c,
    recv_c,
    send_d,
    recv_d,
    send_fw,
    recv_fw,
    send_e,
    recv_e,
    send_f,
    recv_f,
    send_g,
    recv_g,
    send_h,
    recv_h,
    send_i,
    recv_i,
    send_t,
    recv_t,
    send_u,
    recv_u,
):
    n_enc, n_tp = dims
    groups = 2 * n_enc
    enc, mb, tp = lax.axis_index("enc"), lax.axis_index("mb"), lax.axis_index("tp")
    me = enc * 2 + mb
    own, kw = split.shape[1], split.shape[2]
    width = patches.shape[1]
    units = up_w.shape[1]
    cols = down_w.shape[1]
    feats, kv_cols = kv_w.shape
    tokens = text.shape[0]
    seq_rows = n_tp * own
    per_feat = feats // cols
    cuts = [0]
    for size in (width, width, kv_cols, feats, cols, units):
        cuts.append(cuts[-1] + size)
    merge_gain, merge_bias, kv_bias, norm_gain, down_bias, up_bias = (
        params.at[:, start:stop] for start, stop in zip(cuts[:-1], cuts[1:])
    )

    def other_groups():
        for step in range(1, groups):
            to = lax.rem(me + step, groups)
            yield to, {"enc": lax.div(to, 2), "mb": lax.rem(to, 2)}

    def other_encs():
        for step in range(1, n_enc):
            to = lax.rem(enc + step, n_enc)
            yield to, {"enc": to}

    def other_tps():
        for step in range(1, n_tp):
            to = lax.rem(tp + step, n_tp)
            yield to, {"tp": to}

    mate = {"mb": 1 - mb}

    def remote(src, dst, send, recv, to):
        return pltpu.make_async_remote_copy(
            src_ref=src, dst_ref=dst, send_sem=send, recv_sem=recv, device_id=to, device_id_type=MESH
        )

    local = [
        pltpu.make_async_copy(src, dst, local_sem.at[i])
        for i, (src, dst) in enumerate(
            ((up_hbm, up_w), (down_hbm, down_w), (kv_hbm, kv_w), (text_hbm, text))
        )
    ]
    for copy in local:
        copy.start()

    barrier = pltpu.get_barrier_semaphore()
    for _, to in other_groups():
        pl.semaphore_signal(barrier, inc=1, device_id=to, device_id_type=MESH)
    for _, to in other_tps():
        pl.semaphore_signal(barrier, inc=1, device_id=to, device_id_type=MESH)

    def own_part(ref, index, size):
        if ref.shape[0] == size:
            return ref[...]
        return ref[pl.ds(pl.multiple_of(index * size, size), size)]

    merge_gain[...] = gain_in[...][None]
    merge_bias[...] = bias_in[...][None]
    kv_bias[...] = kv_bias_in[...][None]
    norm_gain[...] = own_part(norm_gain_in, tp, feats)[None]
    down_bias[...] = own_part(down_bias_in, me, cols)[None]
    up_bias[...] = own_part(up_bias_in, tp, units)[None]

    values = patches[...].astype(F32)
    center = values - jnp.mean(values, axis=-1, keepdims=True)
    spread = jnp.mean(center * center, axis=-1, keepdims=True)
    normal = (center * lax.rsqrt(spread + 1e-06) * merge_gain[...] + merge_bias[...]).astype(BF16)
    row = lax.broadcasted_iota(jnp.int32, (own, 4 * own), 0)
    column = lax.broadcasted_iota(jnp.int32, (own, 4 * own), 1)
    for j in range(4):
        chosen = jnp.where(column == 4 * row + j, 1.0, 0.0).astype(BF16)
        every = jnp.dot(chosen, normal, preferred_element_type=F32).astype(BF16)
        for piece in range(width // kw):
            split[j * (width // kw) + piece] = every[:, piece * kw : (piece + 1) * kw]
    place_of = lax.broadcasted_iota(jnp.int32, (tokens, seq_rows), 0)
    chosen = jnp.where(place_of == dest[...], 1.0, 0.0)
    picks[...] = chosen.astype(BF16)
    present[...] = jnp.sum(chosen, axis=-1, keepdims=True)
    pl.semaphore_wait(barrier, groups - 1 + n_tp - 1)

    quarter, half = tokens // 4, tokens // 2
    copies_t, copies_u = [], []

    def text_columns(q, of, to, where):
        at = pl.ds(q * quarter, quarter)
        return remote(
            text_hbm.at[at, pl.ds(pl.multiple_of(to * feats, feats), feats)],
            text_cols.at[of, at],
            send_t.at[q, to],
            recv_t.at[q, of],
            where,
        )

    def send_columns(q):
        for to, where in other_tps():
            copy = text_columns(q, tp, to, where)
            copy.start()
            copies_t.append(copy)

    def text_piece(h, src, dst, to, where):
        at = pl.ds(h * half, half)
        return remote(
            text_part.at[src, at], text_in.at[dst, at], send_u.at[h, to], recv_u.at[h, dst], where
        )

    def text_half(h):
        for q in (2 * h, 2 * h + 1):
            for at, where in other_tps():
                text_columns(q, at, at, where).wait_recv()
        span = slice(h * half, (h + 1) * half)
        for at in range(n_tp):
            text_cols[at, span] = (text_cols[at, span].astype(F32) * norm_gain[...]).astype(BF16)
        tile = tiles(kv_cols, 256)

        @pl.loop(0, kv_cols // tile)
        def _(i):
            at = pl.ds(pl.multiple_of(i * tile, tile), tile)
            lhs = text_cols[:, span].reshape(n_tp * half, feats)
            out = jnp.dot(lhs, kv_w[:, at], preferred_element_type=F32)
            text_part[:, span, at] = out.astype(BF16).reshape(n_tp, half, tile)

        for to, where in other_tps():
            copy = text_piece(h, to, tp, to, where)
            copy.start()
            copies_u.append(copy)

    copies_a = []
    for to, where in other_groups():
        copy = remote(split.at[to], rows.at[enc, mb, tp], send_a.at[to], recv_a.at[me], where)
        copy.start()
        copies_a.append(copy)
    send_columns(0)
    rows[enc, mb, tp] = split[me]
    for at, where in other_groups():
        remote(split.at[at], rows.at[lax.div(at, 2), lax.rem(at, 2), tp], send_a.at[at], recv_a.at[at], where).wait_recv()
    copies_b = []
    for to, where in other_tps():
        copy = remote(rows.at[:, :, tp], rows.at[:, :, tp], send_b.at[to], recv_b.at[tp], where)
        copy.start()
        copies_b.append(copy)

    local[0].wait()
    for at, where in other_tps():
        remote(rows.at[:, :, at], rows.at[:, :, at], send_b.at[at], recv_b.at[at], where).wait_recv()

    tile = tiles(units, 256)

    def raise_half(half):
        @pl.loop(0, units // tile)
        def _(i):
            at = pl.ds(pl.multiple_of(i * tile, tile), tile)
            lhs = rows[:, half].reshape(n_enc * seq_rows, kw)
            out = jnp.dot(lhs, up_w[:, at], preferred_element_type=F32)
            part[:, half, :, at] = out.astype(BF16).reshape(n_enc, seq_rows, tile)

    send_columns(1)
    raise_half(1 - mb)
    to_pair = remote(part.at[:, 1 - mb], pair, send_pair, recv_pair, mate)
    to_pair.start()
    raise_half(mb)
    to_pair.wait_recv()
    copies_c = []
    for to, where in other_encs():
        chip_sum[to] = (part[to, mb].astype(F32) + pair[to].astype(F32)).astype(BF16)
        copy = remote(chip_sum.at[to], summed.at[enc], send_c.at[to], recv_c.at[enc], where)
        copy.start()
        copies_c.append(copy)

    send_columns(2)
    send_columns(3)
    local[2].wait()
    local[3].wait()
    text_cols[tp] = text[:, pl.ds(pl.multiple_of(tp * feats, feats), feats)]

    text_half(0)

    total = part[enc, mb].astype(F32) + pair[enc].astype(F32) + up_bias[...]
    for at, where in other_encs():
        remote(chip_sum.at[at], summed.at[at], send_c.at[at], recv_c.at[at], where).wait_recv()
        total = total + summed[at].astype(F32)
    hidden[enc, mb] = (0.5 * total * (1.0 + lax.erf(total * 0.7071067811865476))).astype(BF16)

    copies_d = []
    copy = remote(hidden.at[enc, mb], hidden.at[enc, mb], send_fw.at[enc], recv_fw.at[enc], mate)
    copy.start()
    copies_d.append(copy)
    for to, where in other_encs():
        copy = remote(hidden.at[enc, mb], hidden.at[enc, mb], send_d.at[to], recv_d.at[enc], where)
        copy.start()
        copies_d.append(copy)

    text_half(1)
    for at, where in other_encs():
        remote(hidden.at[at, mb], hidden.at[at, mb], send_d.at[at], recv_d.at[at], where).wait_recv()
        copy = remote(hidden.at[at, mb], hidden.at[at, mb], send_fw.at[at], recv_fw.at[at], mate)
        copy.start()
        copies_d.append(copy)
    for at in range(n_enc):
        remote(
            hidden.at[at, 1 - mb], hidden.at[at, 1 - mb], send_fw.at[at], recv_fw.at[at], mate
        ).wait_recv()

    local[1].wait()
    wide = cols // 2
    copies_e, copies_f = [], []

    def sums_piece(h, to, dst, where):
        at = pl.ds(h * wide, wide)
        return remote(
            lowered.at[:, to, :, at], low_in.at[dst, :, :, at], send_e.at[h, to], recv_e.at[h, dst], where
        )

    for h in range(2):
        at = pl.ds(h * wide, wide)
        lhs = hidden[...].reshape(groups * seq_rows, units)
        out = jnp.dot(lhs, down_w[:, at], preferred_element_type=F32)
        lowered[:, :, :, at] = out.astype(BF16).reshape(groups, n_tp, own, wide)
        for to, where in other_tps():
            copy = sums_piece(h, to, tp, where)
            copy.start()
            copies_e.append(copy)
    low_in[tp] = lowered[:, tp]

    def rows_piece(h, to, of, where):
        at = pl.ds(h * wide, wide)
        return remote(
            vis_part.at[to, :, at], visual.at[tp, of, :, at], send_f.at[h, to], recv_f.at[h, of], where
        )

    for h in range(2):
        at = pl.ds(h * wide, wide)
        for of, where in other_tps():
            sums_piece(h, of, of, where).wait_recv()
        out = low_in[0, :, :, at].astype(F32)
        for t in range(1, n_tp):
            out = out + low_in[t, :, :, at].astype(F32)
        vis_part[:, :, at] = (out + down_bias[:, at]).astype(BF16)
        for to, where in other_groups():
            copy = rows_piece(h, to, me, where)
            copy.start()
            copies_f.append(copy)
    visual[tp, me] = vis_part[me]
    for h in range(2):
        for of, where in other_groups():
            rows_piece(h, of, of, where).wait_recv()

    def visual_piece(of, block, to, where):
        at = visual.at[of, pl.ds(block * per_feat, per_feat)]
        return remote(at, at, send_g.at[to, block], recv_g.at[of, block], where)

    for to, where in other_tps():
        visual_piece(tp, to, to, where).start()
    for at, where in other_tps():
        visual_piece(at, tp, at, where).wait_recv()
    for to, where in other_tps():

        @pl.loop(1, n_tp)
        def _(step):
            visual_piece(tp, lax.rem(to + step, n_tp), to, where).start()

    tile = tiles(kv_cols // 2, 512)
    per_half = kv_cols // 2 // tile
    copies_h, copies_i = [], []

    def vkv_piece(h, to, of, where):
        at = pl.ds(h * (kv_cols // 2), kv_cols // 2)
        return remote(vkv.at[to, :, at], vkv_in.at[of, :, at], send_h.at[h, to], recv_h.at[h, of], where)

    def total_piece(h, to, of, where):
        at = vkv_all.at[of, :, pl.ds(h * (kv_cols // 2), kv_cols // 2)]
        return remote(at, at, send_i.at[h, to], recv_i.at[h, of], where)

    for h in range(2):

        @pl.loop(h * per_half, (h + 1) * per_half)
        def _(i):
            at = pl.ds(pl.multiple_of(i * tile, tile), tile)
            out = jnp.zeros((seq_rows, tile), F32)
            for j in range(per_feat):
                gain = norm_gain[:, j * cols : (j + 1) * cols]
                lhs = visual[:, tp * per_feat + j].reshape(seq_rows, cols)
                lhs = (lhs.astype(F32) * gain).astype(BF16)
                out = out + jnp.dot(
                    lhs, kv_w[j * cols : (j + 1) * cols, at], preferred_element_type=F32
                )
            vkv[:, :, at] = out.astype(BF16).reshape(n_tp, own, tile)

        for to, where in other_tps():
            copy = vkv_piece(h, to, tp, where)
            copy.start()
            copies_h.append(copy)
    vkv_in[tp] = vkv[tp]
    for h in range(2):
        at = pl.ds(h * (kv_cols // 2), kv_cols // 2)
        for of, where in other_tps():
            vkv_piece(h, of, of, where).wait_recv()
        out = vkv_in[0, :, at].astype(F32)
        for t in range(1, n_tp):
            out = out + vkv_in[t, :, at].astype(F32)
        vkv_all[tp, :, at] = out.astype(BF16)
        for to, where in other_tps():
            copy = total_piece(h, to, tp, where)
            copy.start()
            copies_i.append(copy)

    for at, where in other_tps():

        @pl.loop(1, n_tp)
        def _(step):
            visual_piece(at, lax.rem(tp + step, n_tp), at, where).wait_recv()

    def place(i, squares):
        at = pl.ds(pl.multiple_of(i * cols, cols), cols)
        found = jnp.dot(
            picks[...], visual[:, i].reshape(seq_rows, cols), preferred_element_type=F32
        ).astype(BF16).astype(F32)
        mask = jnp.broadcast_to(present[...], (tokens, cols)) > 0.5
        values = jnp.where(mask, found, text[:, at].astype(F32))
        embedded[:, at] = values.astype(BF16)
        return squares + jnp.sum(values * values, axis=-1, keepdims=True)

    squares = lax.fori_loop(0, groups, place, jnp.zeros((tokens, 1), F32))
    scale = lax.rsqrt(squares * (1.0 / (groups * cols)) + 1e-06)

    text_in[tp] = text_part[tp]
    for at, where in other_tps():
        for h in range(2):
            text_piece(h, at, at, at, where).wait_recv()
    for at, where in other_tps():
        for h in range(2):
            total_piece(h, at, at, where).wait_recv()

    @pl.loop(0, kv_cols // tile)
    def _(i):
        at = pl.ds(pl.multiple_of(i * tile, tile), tile)
        found = jnp.dot(
            picks[...], vkv_all[:, :, at].reshape(seq_rows, tile), preferred_element_type=F32
        )
        plain = text_in[0, :, at].astype(F32)
        for t in range(1, n_tp):
            plain = plain + text_in[t, :, at].astype(F32)
        mask = jnp.broadcast_to(present[...], (tokens, tile)) > 0.5
        keys_values[:, at] = (jnp.where(mask, found, plain) * scale + kv_bias[:, at]).astype(BF16)

    to_pair.wait_send()
    for copies in (
        copies_a, copies_b, copies_t, copies_c, copies_d, copies_u,
        copies_e, copies_f, copies_h, copies_i,
    ):
        for copy in copies:
            copy.wait_send()
    for to, where in other_tps():

        @pl.loop(0, n_tp)
        def _(block):
            visual_piece(tp, block, to, where).wait_send()


def per_device(
    patches,
    patch_counts,
    dest_pos,
    merge_gain,
    merge_bias,
    up_weight,
    up_bias,
    down_weight,
    down_bias,
    text_embed,
    norm_gain,
    kv_weight,
    kv_bias,
):
    n_enc, n_tp = lax.axis_size("enc"), lax.axis_size("tp")
    groups = n_enc * lax.axis_size("mb")
    tp = lax.axis_index("tp")
    group = lax.axis_index("enc") * lax.axis_size("mb") + lax.axis_index("mb")
    text = text_embed[0, 0]
    tokens, width = text.shape
    feats, kv_cols = kv_weight.shape
    kw, units = up_weight.shape
    cols = down_weight.shape[1]
    own = patches.shape[2] // 4
    seq_rows = own * n_tp

    live_rows = patch_counts[0, 0] // 4
    live = (jnp.arange(SLOT, dtype=jnp.int32)[None, :] < live_rows[:, None]).reshape(-1)
    dest = (jnp.where(live, dest_pos[0, 0], -1) - tp * tokens)[None]
    up_own = up_bias
    if units % 128:
        up_own = lax.dynamic_slice_in_dim(up_bias, tp * units, units, 0)

    dma = pltpu.SemaphoreType.DMA
    vmem = pl.BlockSpec(memory_space=pltpu.VMEM)
    hbm = pl.BlockSpec(memory_space=pl.ANY)
    by_group, by_enc, by_tp = [dma((groups,))] * 2, [dma((n_enc,))] * 2, [dma((n_tp,))] * 2
    embedded, keys_values = pl.pallas_call(
        functools.partial(kernel, (n_enc, n_tp)),
        out_shape=(
            jax.ShapeDtypeStruct((tokens, width), BF16),
            jax.ShapeDtypeStruct((tokens, kv_cols), BF16),
        ),
        in_specs=[vmem] * 8 + [hbm] * 4,
        out_specs=(vmem, vmem),
        scratch_shapes=[
            pltpu.VMEM((kw, units), BF16),
            pltpu.VMEM((units, cols), BF16),
            pltpu.VMEM((feats, kv_cols), BF16),
            pltpu.VMEM((tokens, width), BF16),
            pltpu.VMEM((groups, own, kw), BF16),
            pltpu.VMEM((n_enc, 2, n_tp, own, kw), BF16),
            pltpu.VMEM((n_enc, 2, seq_rows, units), BF16),
            pltpu.VMEM((n_enc, seq_rows, units), BF16),
            pltpu.VMEM((n_enc, seq_rows, units), BF16),
            pltpu.VMEM((n_enc, seq_rows, units), BF16),
            pltpu.VMEM((n_enc, 2, seq_rows, units), BF16),
            pltpu.VMEM((groups, n_tp, own, cols), BF16),
            pltpu.VMEM((n_tp, groups, own, cols), BF16),
            pltpu.VMEM((groups, own, cols), BF16),
            pltpu.VMEM((n_tp, groups, own, cols), BF16),
            pltpu.VMEM((n_tp, own, kv_cols), BF16),
            pltpu.VMEM((n_tp, own, kv_cols), BF16),
            pltpu.VMEM((n_tp, own, kv_cols), BF16),
            pltpu.VMEM((n_tp, tokens, feats), BF16),
            pltpu.VMEM((n_tp, tokens, kv_cols), BF16),
            pltpu.VMEM((n_tp, tokens, kv_cols), BF16),
            pltpu.VMEM((tokens, seq_rows), BF16),
            pltpu.VMEM((tokens, 1), F32),
            pltpu.VMEM((1, 2 * patches.shape[3] + kv_cols + feats + cols + units), F32),
            dma((4,)),
        ]
        + by_group + by_tp + [dma, dma] + by_enc + by_enc + by_enc
        + [dma((2, n_tp))] * 2 + [dma((2, groups))] * 2 + [dma((n_tp, n_tp))] * 2 + [dma((2, n_tp))] * 4
        + [dma((4, n_tp))] * 2 + [dma((2, n_tp))] * 2,
        compiler_params=pltpu.CompilerParams(
            collective_id=0, has_side_effects=True, vmem_limit_bytes=60 * 1024 * 1024
        ),
        cost_estimate=pl.CostEstimate(
            flops=2 * groups * seq_rows * units * (kw + cols) + 2 * n_tp * tokens * feats * kv_cols,
            bytes_accessed=2 * (kw * units + units * cols + feats * kv_cols + 2 * tokens * width),
            transcendentals=seq_rows * units,
        ),
    )(
        patches[0, 0],
        merge_gain,
        merge_bias,
        kv_bias,
        norm_gain,
        down_bias,
        up_own,
        dest,
        up_weight,
        down_weight,
        kv_weight,
        text,
    )
    return (embedded[None, None], keys_values[None, None])


def solution(mesh):
    return jax.shard_map(
        per_device,
        mesh=mesh,
        in_specs=(
            P("enc", "mb", "tp", None),
            P("enc", "mb", None),
            P("enc", "mb", None),
            P(),
            P(),
            P(("enc", "mb"), "tp"),
            P(),
            P("tp", ("enc", "mb")),
            P(),
            P("enc", "mb", "tp", None),
            P(),
            P("tp", None),
            P(),
        ),
        out_specs=(P("enc", "mb", "tp", None), P("enc", "mb", "tp", None)),
        check_vma=False,
    )
```

```python
import functools

import jax
import jax.numpy as jnp
from jax import lax
from jax.experimental import pallas as pl
from jax.experimental.pallas import tpu as pltpu
from jax.sharding import PartitionSpec as P

SLOT = 8
F32 = jnp.float32
BF16 = jnp.bfloat16
MESH = pl.DeviceIdType.MESH


def tiles(width, tile):
    return tile if width % tile == 0 else width


def kernel(
    dims,
    patches,
    gain_in,
    bias_in,
    kv_bias_in,
    norm_gain_in,
    down_bias_in,
    up_bias_in,
    dest,
    up_hbm,
    down_hbm,
    kv_hbm,
    text_hbm,
    embedded,
    keys_values,
    up_w,
    down_w,
    kv_w,
    text,
    split,
    rows,
    part,
    pair,
    chip_sum,
    summed,
    hidden,
    lowered,
    low_in,
    vis_part,
    visual,
    vkv,
    vkv_in,
    vkv_all,
    text_cols,
    text_part,
    text_in,
    picks,
    present,
    params,
    local_sem,
    send_a,
    recv_a,
    send_b,
    recv_b,
    send_pair,
    recv_pair,
    send_c,
    recv_c,
    send_d,
    recv_d,
    send_fw,
    recv_fw,
    send_e,
    recv_e,
    send_f,
    recv_f,
    send_g,
    recv_g,
    send_h,
    recv_h,
    send_i,
    recv_i,
    send_t,
    recv_t,
    send_u,
    recv_u,
):
    n_enc, n_tp = dims
    groups = 2 * n_enc
    enc, mb, tp = lax.axis_index("enc"), lax.axis_index("mb"), lax.axis_index("tp")
    me = enc * 2 + mb
    own, kw = split.shape[1], split.shape[2]
    width = patches.shape[1]
    units = up_w.shape[1]
    cols = down_w.shape[1]
    feats, kv_cols = kv_w.shape
    tokens = text.shape[0]
    seq_rows = n_tp * own
    per_feat = feats // cols
    cuts = [0]
    for size in (width, width, kv_cols, feats, cols, units):
        cuts.append(cuts[-1] + size)
    merge_gain, merge_bias, kv_bias, norm_gain, down_bias, up_bias = (
        params.at[:, start:stop] for start, stop in zip(cuts[:-1], cuts[1:])
    )

    def other_groups():
        for step in range(1, groups):
            to = lax.rem(me + step, groups)
            yield to, {"enc": lax.div(to, 2), "mb": lax.rem(to, 2)}

    def other_encs():
        for step in range(1, n_enc):
            to = lax.rem(enc + step, n_enc)
            yield to, {"enc": to}

    def other_tps():
        for step in range(1, n_tp):
            to = lax.rem(tp + step, n_tp)
            yield to, {"tp": to}

    mate = {"mb": 1 - mb}

    def remote(src, dst, send, recv, to):
        return pltpu.make_async_remote_copy(
            src_ref=src, dst_ref=dst, send_sem=send, recv_sem=recv, device_id=to, device_id_type=MESH
        )

    local = [
        pltpu.make_async_copy(src, dst, local_sem.at[i])
        for i, (src, dst) in enumerate(
            ((up_hbm, up_w), (down_hbm, down_w), (kv_hbm, kv_w), (text_hbm, text))
        )
    ]
    for copy in local:
        copy.start()

    barrier = pltpu.get_barrier_semaphore()
    for _, to in other_groups():
        pl.semaphore_signal(barrier, inc=1, device_id=to, device_id_type=MESH)
    for _, to in other_tps():
        pl.semaphore_signal(barrier, inc=1, device_id=to, device_id_type=MESH)

    def own_part(ref, index, size):
        if ref.shape[0] == size:
            return ref[...]
        return ref[pl.ds(pl.multiple_of(index * size, size), size)]

    merge_gain[...] = gain_in[...][None]
    merge_bias[...] = bias_in[...][None]
    kv_bias[...] = kv_bias_in[...][None]
    norm_gain[...] = own_part(norm_gain_in, tp, feats)[None]
    down_bias[...] = own_part(down_bias_in, me, cols)[None]
    up_bias[...] = own_part(up_bias_in, tp, units)[None]

    values = patches[...].astype(F32)
    center = values - jnp.mean(values, axis=-1, keepdims=True)
    spread = jnp.mean(center * center, axis=-1, keepdims=True)
    normal = (center * lax.rsqrt(spread + 1e-06) * merge_gain[...] + merge_bias[...]).astype(BF16)
    row = lax.broadcasted_iota(jnp.int32, (own, 4 * own), 0)
    column = lax.broadcasted_iota(jnp.int32, (own, 4 * own), 1)
    for j in range(4):
        chosen = jnp.where(column == 4 * row + j, 1.0, 0.0).astype(BF16)
        every = jnp.dot(chosen, normal, preferred_element_type=F32).astype(BF16)
        for piece in range(width // kw):
            split[j * (width // kw) + piece] = every[:, piece * kw : (piece + 1) * kw]
    place_of = lax.broadcasted_iota(jnp.int32, (tokens, seq_rows), 0)
    chosen = jnp.where(place_of == dest[...], 1.0, 0.0)
    picks[...] = chosen.astype(BF16)
    present[...] = jnp.sum(chosen, axis=-1, keepdims=True)
    pl.semaphore_wait(barrier, groups - 1 + n_tp - 1)

    quarter, half = tokens // 4, tokens // 2
    copies_t, copies_u = [], []

    def text_columns(q, of, to, where):
        at = pl.ds(q * quarter, quarter)
        return remote(
            text_hbm.at[at, pl.ds(pl.multiple_of(to * feats, feats), feats)],
            text_cols.at[of, at],
            send_t.at[q, to],
            recv_t.at[q, of],
            where,
        )

    def send_columns(q):
        for to, where in other_tps():
            copy = text_columns(q, tp, to, where)
            copy.start()
            copies_t.append(copy)

    def text_piece(h, src, dst, to, where):
        at = pl.ds(h * half, half)
        return remote(
            text_part.at[src, at], text_in.at[dst, at], send_u.at[h, to], recv_u.at[h, dst], where
        )

    def text_half(h):
        for q in (2 * h, 2 * h + 1):
            for at, where in other_tps():
                text_columns(q, at, at, where).wait_recv()
        span = slice(h * half, (h + 1) * half)
        for at in range(n_tp):
            text_cols[at, span] = (text_cols[at, span].astype(F32) * norm_gain[...]).astype(BF16)
        tile = tiles(kv_cols, 256)

        @pl.loop(0, kv_cols // tile)
        def _(i):
            at = pl.ds(pl.multiple_of(i * tile, tile), tile)
            lhs = text_cols[:, span].reshape(n_tp * half, feats)
            out = jnp.dot(lhs, kv_w[:, at], preferred_element_type=F32)
            text_part[:, span, at] = out.astype(BF16).reshape(n_tp, half, tile)

        for to, where in other_tps():
            copy = text_piece(h, to, tp, to, where)
            copy.start()
            copies_u.append(copy)

    copies_a = []
    for to, where in other_groups():
        copy = remote(split.at[to], rows.at[enc, mb, tp], send_a.at[to], recv_a.at[me], where)
        copy.start()
        copies_a.append(copy)
    send_columns(0)
    rows[enc, mb, tp] = split[me]
    for at, where in other_groups():
        remote(split.at[at], rows.at[lax.div(at, 2), lax.rem(at, 2), tp], send_a.at[at], recv_a.at[at], where).wait_recv()
    copies_b = []
    for to, where in other_tps():
        copy = remote(rows.at[:, :, tp], rows.at[:, :, tp], send_b.at[to], recv_b.at[tp], where)
        copy.start()
        copies_b.append(copy)

    local[0].wait()
    for at, where in other_tps():
        remote(rows.at[:, :, at], rows.at[:, :, at], send_b.at[at], recv_b.at[at], where).wait_recv()

    send_columns(1)
    n_cut = 2 if units % 256 == 0 else 1
    unit_cuts = [pl.ds(u * (units // n_cut), units // n_cut) for u in range(n_cut)]
    pair_copies = []
    for u, at in enumerate(unit_cuts):
        for half_at in (1 - mb, mb):
            lhs = rows[:, half_at].reshape(n_enc * seq_rows, kw)
            out = jnp.dot(lhs, up_w[:, at], preferred_element_type=F32)
            part[:, half_at, :, at] = out.astype(BF16).reshape(n_enc, seq_rows, units // n_cut)
            if len(pair_copies) == u:
                copy = remote(
                    part.at[:, 1 - mb, :, at], pair.at[:, :, at], send_pair.at[u], recv_pair.at[u], mate
                )
                copy.start()
                pair_copies.append(copy)

    def sum_piece(u, to, of, where):
        at = unit_cuts[u]
        return remote(
            chip_sum.at[to, :, at], summed.at[of, :, at], send_c.at[u, to], recv_c.at[u, of], where
        )

    copies_c = []
    for u, at in enumerate(unit_cuts):
        pair_copies[u].wait_recv()
        for to, where in other_encs():
            chip_sum[to, :, at] = (part[to, mb, :, at].astype(F32) + pair[to, :, at].astype(F32)).astype(BF16)
            copy = sum_piece(u, to, enc, where)
            copy.start()
            copies_c.append(copy)

    send_columns(2)
    send_columns(3)
    local[2].wait()
    local[3].wait()
    text_cols[tp] = text[:, pl.ds(pl.multiple_of(tp * feats, feats), feats)]

    text_half(0)

    def hidden_piece(u, of_enc, of_mb, send, recv, to, where):
        at = hidden.at[of_enc, of_mb, :, unit_cuts[u]]
        return remote(at, at, send.at[u, to], recv.at[u, of_enc], where)

    copies_d = []
    for u, at in enumerate(unit_cuts):
        total = part[enc, mb, :, at].astype(F32) + pair[enc, :, at].astype(F32) + up_bias[:, at]
        for of, where in other_encs():
            sum_piece(u, of, of, where).wait_recv()
            total = total + summed[of, :, at].astype(F32)
        hidden[enc, mb, :, at] = (0.5 * total * (1.0 + lax.erf(total * 0.7071067811865476))).astype(BF16)
        for to, where in other_encs():
            copy = hidden_piece(u, enc, mb, send_d, recv_d, to, where)
            copy.start()
            copies_d.append(copy)
        copy = hidden_piece(u, enc, mb, send_fw, recv_fw, enc, mate)
        copy.start()
        copies_d.append(copy)

    text_half(1)
    for u in range(n_cut):
        for of, where in other_encs():
            hidden_piece(u, of, mb, send_d, recv_d, of, where).wait_recv()
            copy = hidden_piece(u, of, mb, send_fw, recv_fw, of, mate)
            copy.start()
            copies_d.append(copy)
    for u in range(n_cut):
        for of in range(n_enc):
            hidden_piece(u, of, 1 - mb, send_fw, recv_fw, of, mate).wait_recv()

    local[1].wait()
    wide = cols // 2
    copies_e, copies_f = [], []

    def sums_piece(h, to, dst, where):
        at = pl.ds(h * wide, wide)
        return remote(
            lowered.at[:, to, :, at], low_in.at[dst, :, :, at], send_e.at[h, to], recv_e.at[h, dst], where
        )

    for h in range(2):
        at = pl.ds(h * wide, wide)
        lhs = hidden[...].reshape(groups * seq_rows, units)
        out = jnp.dot(lhs, down_w[:, at], preferred_element_type=F32)
        lowered[:, :, :, at] = out.astype(BF16).reshape(groups, n_tp, own, wide)
        for to, where in other_tps():
            copy = sums_piece(h, to, tp, where)
            copy.start()
            copies_e.append(copy)
    low_in[tp] = lowered[:, tp]

    def rows_piece(h, to, of, where):
        at = pl.ds(h * wide, wide)
        return remote(
            vis_part.at[to, :, at], visual.at[tp, of, :, at], send_f.at[h, to], recv_f.at[h, of], where
        )

    for h in range(2):
        at = pl.ds(h * wide, wide)
        for of, where in other_tps():
            sums_piece(h, of, of, where).wait_recv()
        out = low_in[0, :, :, at].astype(F32)
        for t in range(1, n_tp):
            out = out + low_in[t, :, :, at].astype(F32)
        vis_part[:, :, at] = (out + down_bias[:, at]).astype(BF16)
        for to, where in other_groups():
            copy = rows_piece(h, to, me, where)
            copy.start()
            copies_f.append(copy)
    visual[tp, me] = vis_part[me]
    for h in range(2):
        for of, where in other_groups():
            rows_piece(h, of, of, where).wait_recv()

    def visual_piece(of, block, to, where):
        at = visual.at[of, pl.ds(block * per_feat, per_feat)]
        return remote(at, at, send_g.at[to, block], recv_g.at[of, block], where)

    for to, where in other_tps():
        visual_piece(tp, to, to, where).start()
    for at, where in other_tps():
        visual_piece(at, tp, at, where).wait_recv()
    for to, where in other_tps():

        @pl.loop(1, n_tp)
        def _(step):
            visual_piece(tp, lax.rem(to + step, n_tp), to, where).start()

    tile = tiles(kv_cols // 2, 512)
    per_half = kv_cols // 2 // tile
    copies_h, copies_i = [], []

    def vkv_piece(h, to, of, where):
        at = pl.ds(h * (kv_cols // 2), kv_cols // 2)
        return remote(vkv.at[to, :, at], vkv_in.at[of, :, at], send_h.at[h, to], recv_h.at[h, of], where)

    def total_piece(h, to, of, where):
        at = vkv_all.at[of, :, pl.ds(h * (kv_cols // 2), kv_cols // 2)]
        return remote(at, at, send_i.at[h, to], recv_i.at[h, of], where)

    for h in range(2):

        @pl.loop(h * per_half, (h + 1) * per_half)
        def _(i):
            at = pl.ds(pl.multiple_of(i * tile, tile), tile)
            out = jnp.zeros((seq_rows, tile), F32)
            for j in range(per_feat):
                gain = norm_gain[:, j * cols : (j + 1) * cols]
                lhs = visual[:, tp * per_feat + j].reshape(seq_rows, cols)
                lhs = (lhs.astype(F32) * gain).astype(BF16)
                out = out + jnp.dot(
                    lhs, kv_w[j * cols : (j + 1) * cols, at], preferred_element_type=F32
                )
            vkv[:, :, at] = out.astype(BF16).reshape(n_tp, own, tile)

        for to, where in other_tps():
            copy = vkv_piece(h, to, tp, where)
            copy.start()
            copies_h.append(copy)
    vkv_in[tp] = vkv[tp]
    for h in range(2):
        at = pl.ds(h * (kv_cols // 2), kv_cols // 2)
        for of, where in other_tps():
            vkv_piece(h, of, of, where).wait_recv()
        out = vkv_in[0, :, at].astype(F32)
        for t in range(1, n_tp):
            out = out + vkv_in[t, :, at].astype(F32)
        vkv_all[tp, :, at] = out.astype(BF16)
        for to, where in other_tps():
            copy = total_piece(h, to, tp, where)
            copy.start()
            copies_i.append(copy)

    for at, where in other_tps():

        @pl.loop(1, n_tp)
        def _(step):
            visual_piece(at, lax.rem(tp + step, n_tp), at, where).wait_recv()

    def place(i, squares):
        at = pl.ds(pl.multiple_of(i * cols, cols), cols)
        found = jnp.dot(
            picks[...], visual[:, i].reshape(seq_rows, cols), preferred_element_type=F32
        ).astype(BF16).astype(F32)
        mask = jnp.broadcast_to(present[...], (tokens, cols)) > 0.5
        values = jnp.where(mask, found, text[:, at].astype(F32))
        embedded[:, at] = values.astype(BF16)
        return squares + jnp.sum(values * values, axis=-1, keepdims=True)

    squares = lax.fori_loop(0, groups, place, jnp.zeros((tokens, 1), F32))
    scale = lax.rsqrt(squares * (1.0 / (groups * cols)) + 1e-06)

    text_in[tp] = text_part[tp]
    for at, where in other_tps():
        for h in range(2):
            text_piece(h, at, at, at, where).wait_recv()
    for at, where in other_tps():
        for h in range(2):
            total_piece(h, at, at, where).wait_recv()

    @pl.loop(0, kv_cols // tile)
    def _(i):
        at = pl.ds(pl.multiple_of(i * tile, tile), tile)
        found = jnp.dot(
            picks[...], vkv_all[:, :, at].reshape(seq_rows, tile), preferred_element_type=F32
        )
        plain = text_in[0, :, at].astype(F32)
        for t in range(1, n_tp):
            plain = plain + text_in[t, :, at].astype(F32)
        mask = jnp.broadcast_to(present[...], (tokens, tile)) > 0.5
        keys_values[:, at] = (jnp.where(mask, found, plain) * scale + kv_bias[:, at]).astype(BF16)

    for copies in (
        pair_copies, copies_a, copies_b, copies_t, copies_c, copies_d, copies_u,
        copies_e, copies_f, copies_h, copies_i,
    ):
        for copy in copies:
            copy.wait_send()
    for to, where in other_tps():

        @pl.loop(0, n_tp)
        def _(block):
            visual_piece(tp, block, to, where).wait_send()


def per_device(
    patches,
    patch_counts,
    dest_pos,
    merge_gain,
    merge_bias,
    up_weight,
    up_bias,
    down_weight,
    down_bias,
    text_embed,
    norm_gain,
    kv_weight,
    kv_bias,
):
    n_enc, n_tp = lax.axis_size("enc"), lax.axis_size("tp")
    groups = n_enc * lax.axis_size("mb")
    tp = lax.axis_index("tp")
    group = lax.axis_index("enc") * lax.axis_size("mb") + lax.axis_index("mb")
    text = text_embed[0, 0]
    tokens, width = text.shape
    feats, kv_cols = kv_weight.shape
    kw, units = up_weight.shape
    cols = down_weight.shape[1]
    own = patches.shape[2] // 4
    seq_rows = own * n_tp

    live_rows = patch_counts[0, 0] // 4
    live = (jnp.arange(SLOT, dtype=jnp.int32)[None, :] < live_rows[:, None]).reshape(-1)
    dest = (jnp.where(live, dest_pos[0, 0], -1) - tp * tokens)[None]
    up_own = up_bias
    if units % 128:
        up_own = lax.dynamic_slice_in_dim(up_bias, tp * units, units, 0)

    dma = pltpu.SemaphoreType.DMA
    vmem = pl.BlockSpec(memory_space=pltpu.VMEM)
    hbm = pl.BlockSpec(memory_space=pl.ANY)
    n_cut = 2 if units % 256 == 0 else 1
    by_group, by_tp = [dma((groups,))] * 2, [dma((n_tp,))] * 2
    embedded, keys_values = pl.pallas_call(
        functools.partial(kernel, (n_enc, n_tp)),
        out_shape=(
            jax.ShapeDtypeStruct((tokens, width), BF16),
            jax.ShapeDtypeStruct((tokens, kv_cols), BF16),
        ),
        in_specs=[vmem] * 8 + [hbm] * 4,
        out_specs=(vmem, vmem),
        scratch_shapes=[
            pltpu.VMEM((kw, units), BF16),
            pltpu.VMEM((units, cols), BF16),
            pltpu.VMEM((feats, kv_cols), BF16),
            pltpu.VMEM((tokens, width), BF16),
            pltpu.VMEM((groups, own, kw), BF16),
            pltpu.VMEM((n_enc, 2, n_tp, own, kw), BF16),
            pltpu.VMEM((n_enc, 2, seq_rows, units), BF16),
            pltpu.VMEM((n_enc, seq_rows, units), BF16),
            pltpu.VMEM((n_enc, seq_rows, units), BF16),
            pltpu.VMEM((n_enc, seq_rows, units), BF16),
            pltpu.VMEM((n_enc, 2, seq_rows, units), BF16),
            pltpu.VMEM((groups, n_tp, own, cols), BF16),
            pltpu.VMEM((n_tp, groups, own, cols), BF16),
            pltpu.VMEM((groups, own, cols), BF16),
            pltpu.VMEM((n_tp, groups, own, cols), BF16),
            pltpu.VMEM((n_tp, own, kv_cols), BF16),
            pltpu.VMEM((n_tp, own, kv_cols), BF16),
            pltpu.VMEM((n_tp, own, kv_cols), BF16),
            pltpu.VMEM((n_tp, tokens, feats), BF16),
            pltpu.VMEM((n_tp, tokens, kv_cols), BF16),
            pltpu.VMEM((n_tp, tokens, kv_cols), BF16),
            pltpu.VMEM((tokens, seq_rows), BF16),
            pltpu.VMEM((tokens, 1), F32),
            pltpu.VMEM((1, 2 * patches.shape[3] + kv_cols + feats + cols + units), F32),
            dma((4,)),
        ]
        + by_group + by_tp + [dma((n_cut,))] * 2 + [dma((n_cut, n_enc))] * 6
        + [dma((2, n_tp))] * 2 + [dma((2, groups))] * 2 + [dma((n_tp, n_tp))] * 2 + [dma((2, n_tp))] * 4
        + [dma((4, n_tp))] * 2 + [dma((2, n_tp))] * 2,
        compiler_params=pltpu.CompilerParams(
            collective_id=0, has_side_effects=True, vmem_limit_bytes=60 * 1024 * 1024
        ),
        cost_estimate=pl.CostEstimate(
            flops=2 * groups * seq_rows * units * (kw + cols) + 2 * n_tp * tokens * feats * kv_cols,
            bytes_accessed=2 * (kw * units + units * cols + feats * kv_cols + 2 * tokens * width),
            transcendentals=seq_rows * units,
        ),
    )(
        patches[0, 0],
        merge_gain,
        merge_bias,
        kv_bias,
        norm_gain,
        down_bias,
        up_own,
        dest,
        up_weight,
        down_weight,
        kv_weight,
        text,
    )
    return (embedded[None, None], keys_values[None, None])


def solution(mesh):
    return jax.shard_map(
        per_device,
        mesh=mesh,
        in_specs=(
            P("enc", "mb", "tp", None),
            P("enc", "mb", None),
            P("enc", "mb", None),
            P(),
            P(),
            P(("enc", "mb"), "tp"),
            P(),
            P("tp", ("enc", "mb")),
            P(),
            P("enc", "mb", "tp", None),
            P(),
            P("tp", None),
            P(),
        ),
        out_specs=(P("enc", "mb", "tp", None), P("enc", "mb", "tp", None)),
        check_vma=False,
    )
```
